32 devices in a mesh: slides: 2 (over y), rows: 8 (over z, x), cols: 2 (over core).
Axes of the slice: x: 2, y: 2, z: 4, core: 2. Of those that a mesh axis runs over, the one named last changes fastest.
Arguments:
- tokens: bfloat16 [512, 32, 512], P(('slides', 'cols'), 'rows'), parts along dimension 0, may hold values from -6 to 6
- norm_gain: float32 [512], replicated, may hold values from 0.5 to 1.5
- w_in: bfloat16 [512, 2048], replicated, may hold values from -0.25 to 0.25
- w_bc: bfloat16 [512, 64], replicated, may hold values from -0.046875 to 0.046875
- rate_row: float32 [16, 1024], replicated, may hold values from 0.002 to 0.08
- rate_col: float32 [16, 1024], replicated, may hold values from 0.002 to 0.08
- skip_gain: float32 [1024], replicated, may hold values from 0.5 to 1.5
- w_out: bfloat16 [1024, 512], replicated, may hold values from -0.1875 to 0.1875
Outputs:
- mixed: bfloat16 [512, 32, 512], P(('slides', 'cols'), 'rows'), parts along dimension 0
The draws below stay inside these ranges and needn't reach their ends.
There are 2 independent parts, one for each index of `slides`. The reference program is written for one: setup_inputs(seed, part) draws one part's arguments, and reference() takes and returns one part's arrays. A program takes and returns all parts, laid end to end along the dimension named above; an argument that names none is the same for every part. Nothing has to cross between parts.
All inputs are finite; a program needn't handle non-finite values.
Results may differ from the reference program's by a relative error of at most 0.013.
Values may be sent and summed in bfloat16 or wider, within the bound.
No kernel may reach another device: no remote copies, remote signals or barrier semaphores. Data moves between devices by JAX's collectives and lax.ppermute only.
A program may use at most 64 MiB of HBM per device.

```python
import math
import jax
import jax.numpy as jnp
from jax import lax

D = 512
E = 1024
N = 16
H = 256
W = 32


def block_levels(stream_key, extent, split, least, top_value):
    factor_of = 1.0
    for position, parts in split:
        draws = jax.random.uniform(jax.random.fold_in(jax.random.fold_in(stream_key, 6), position), (parts,), jnp.float32, least / len(split), top_value / len(split))
        factor_of = factor_of * jnp.repeat(jnp.exp(draws), extent[position] // parts).reshape((-1,) + (1,) * (len(extent) - 1 - position))
    return factor_of


def centred(own_key, dims, deviation, limit, cuts=(), dtype=jnp.bfloat16):
    entries = jax.random.normal(own_key, dims, jnp.float32) * deviation
    if len(cuts) > 0:
        entries = block_levels(own_key, dims, cuts, -0.22, 0.18) * entries
    return jnp.clip(entries, min=-limit, max=limit).astype(dtype)


def setup_inputs(seed: int = 0, part: int = 0) -> dict:
    arg_keys = jax.random.split(jax.random.key(seed), 9)
    own_keys = jax.random.split(jax.random.fold_in(arg_keys[8], part), 9)
    tokens = centred(own_keys[0], (H, W, D), 1.0, 6.0, ((0, 2), (1, 8)))
    norm_gain = jnp.clip(1.0 + 0.1 * jax.random.normal(arg_keys[1], (D,), jnp.float32), 0.5, 1.5)
    w_in = centred(arg_keys[2], (D, 2 * E), D ** -0.5, 0.25)
    w_bc = centred(arg_keys[3], (D, 4 * N), (32 * D) ** -0.5, 0.046875)
    rate_row = jnp.clip(jnp.exp(jax.random.uniform(arg_keys[4], (N, E), jnp.float32, math.log(0.002), math.log(0.08))), 0.002, 0.08)
    rate_col = jnp.clip(jnp.exp(jax.random.uniform(arg_keys[5], (N, E), jnp.float32, math.log(0.002), math.log(0.08))), 0.002, 0.08)
    skip_gain = jnp.clip(jax.random.uniform(arg_keys[6], (E,), jnp.float32, 0.5, 1.5), 0.5, 1.5)
    w_out = centred(arg_keys[7], (E, D), E ** -0.5, 0.1875)
    return {"tokens": tokens, "norm_gain": norm_gain, "w_in": w_in, "w_bc": w_bc, "rate_row": rate_row, "rate_col": rate_col, "skip_gain": skip_gain, "w_out": w_out}


def run_scan(series, inject, readout, rate, skip_weight):
    decay_factor = jnp.exp(-rate)

    def advance(carried, inputs):
        value_now, inject_now, read_now = inputs
        carried = decay_factor[None] * carried + inject_now[:, :, None] * value_now[:, None, :]
        result = jnp.einsum('ine,in->ie', carried, read_now, precision=lax.Precision.HIGHEST) + skip_weight * value_now
        return (carried, result)
    start_state = jnp.zeros((series.shape[1], rate.shape[0], rate.shape[1]), jnp.float32)
    _, results = lax.scan(advance, start_state, (series, inject, readout))
    return results

def reference(tokens, norm_gain, w_in, w_bc, rate_row, rate_col, skip_gain, w_out):
    inner_width = w_out.shape[0]
    state_width = rate_row.shape[0]
    as_float = tokens.astype(jnp.float32)
    scale_now = lax.rsqrt(lax.optimization_barrier(jnp.mean(as_float * as_float, axis=-1, keepdims=True)) + 1e-05)
    normed = (as_float * scale_now * norm_gain).astype(jnp.bfloat16)
    project = jnp.dot(normed, w_in, preferred_element_type=jnp.float32)
    inputs_u = lax.optimization_barrier(project[..., :inner_width].astype(jnp.bfloat16)).astype(jnp.float32)
    gate_z = lax.optimization_barrier(project[..., inner_width:].astype(jnp.bfloat16)).astype(jnp.float32)
    mixers = lax.optimization_barrier(jnp.dot(normed, w_bc, preferred_element_type=jnp.float32).astype(jnp.bfloat16)).astype(jnp.float32)
    b_row = mixers[..., :state_width]
    c_row = mixers[..., state_width:2 * state_width]
    b_col = mixers[..., 2 * state_width:3 * state_width]
    c_col = mixers[..., 3 * state_width:]
    along_rows = run_scan(inputs_u.transpose(1, 0, 2), b_row.transpose(1, 0, 2), c_row.transpose(1, 0, 2), rate_row, skip_gain)
    along_rows = along_rows.transpose(1, 0, 2)
    row_mixed = lax.optimization_barrier(along_rows.astype(jnp.bfloat16)).astype(jnp.float32)
    col_mixed = run_scan(row_mixed, b_col, c_col, rate_col, 1.0)
    gated = (col_mixed * jax.nn.silu(gate_z)).astype(jnp.bfloat16)
    return jnp.dot(gated, w_out, preferred_element_type=jnp.float32).astype(jnp.bfloat16)
```

```python
import functools

import jax
import jax.numpy as jnp
import numpy as np
from jax import lax
from jax.experimental import pallas as pl
from jax.experimental.pallas import tpu as pltpu
from jax.sharding import PartitionSpec as P

F32 = jnp.float32
BF16 = jnp.bfloat16
VMEM = pl.BlockSpec(memory_space=pltpu.VMEM)
LANES = 128


def normalise(tokens, gain):
    as_float = tokens.astype(F32)
    scale_now = lax.rsqrt(jnp.mean(as_float * as_float, axis=-1, keepdims=True) + 1e-05)
    return (as_float * scale_now * gain).astype(BF16)


def dot(a, b):
    return jnp.dot(a, b, preferred_element_type=F32)


def params():
    return pltpu.CompilerParams(vmem_limit_bytes=40 << 20)


def selection(shape, sources):
    matrix = np.zeros(shape, np.float32)
    matrix[np.arange(shape[0]), sources] = 1.0
    return jnp.asarray(matrix, BF16)


def row_order(items, columns):
    c, i = np.divmod(np.arange(items * columns), items)
    return selection((items * columns,) * 2, i * columns + c)


def spread_order(items, folds, columns):
    i, rest = np.divmod(np.arange(items * folds * columns), folds * columns)
    return selection((items * folds * columns,) * 2, rest * items + i)


def repeat_order(items, folds, columns):
    i, rest = np.divmod(np.arange(items * folds * columns), folds * columns)
    return selection((items * folds * columns, items * columns), i * columns + rest % columns)


def gather_order(items, folds, columns):
    f, rest = np.divmod(np.arange(items * folds * columns), items * columns)
    i, c = np.divmod(rest, columns)
    return selection((items * folds * columns,) * 2, (i * folds + f) * columns + c)


def lane_table(state):
    return jnp.asarray(np.repeat(np.eye(state, dtype=np.float32), LANES, axis=1), BF16)


def row_kernel(parts, items, columns, x_ref, gain_ref, wu_ref, wb_ref, wc_ref, rate_ref, skip_ref,
               order_ref, spread_ref, out_ref, normed, b_scr, c_scr, u_scr, y_scr, g_scr):
    block = items * columns
    steps = parts * columns
    rows = steps * items
    inner = u_scr.shape[1]
    folds = spread_ref.shape[0] // block
    gain = gain_ref[...]
    for part in range(parts):
        here = normalise(x_ref[part], gain)
        normed[part * block:(part + 1) * block, :] = dot(order_ref[...], here).astype(BF16)
    b_scr[...] = dot(normed[...], wb_ref[...]).astype(BF16).astype(F32)
    c_scr[...] = dot(normed[...], wc_ref[...]).astype(BF16).astype(F32)
    chunk = 128
    pieces = []
    at = 0
    for lag in range(steps):
        first = lag * items
        while first < rows:
            count = min(chunk, rows - first)
            pieces.append((lag, first, count, at))
            first += count
            at += count
    for lag, first, count, at in pieces:
        source = first - lag * items
        product = c_scr[first:first + count, :] * b_scr[source:source + count, :]
        g_scr[at:at + count, :] = product.astype(BF16)
    tile = 512

    def one_tile(tile_id, _):
        where = pl.ds(pl.multiple_of(tile_id * tile, tile), tile)
        u_scr[:, where] = dot(normed[...], wu_ref[:, where]).astype(BF16).astype(F32)
        rate = rate_ref[:, where]
        skip = skip_ref[:, where]
        done = -1
        table = None
        for lag, first, count, at in pieces:
            if lag != done:
                power = jnp.exp(rate * (-float(lag)))
                high = power.astype(BF16)
                low = (power - high.astype(F32)).astype(BF16)
                table = jnp.concatenate([high, low], axis=0)
                done = lag
            matrix = dot(g_scr[at:at + count, :], table)
            source = first - lag * items
            value = u_scr[source:source + count, where]
            if lag == 0:
                y_scr[first:first + count, where] = (matrix + skip) * value
            else:
                y_scr[first:first + count, where] += matrix * value
        return 0

    lax.fori_loop(0, inner // tile, one_tile, 0)
    width = inner // folds
    for part in range(parts):
        here = slice(part * block, (part + 1) * block)
        stacked = jnp.concatenate(
            [y_scr[here, f * width:(f + 1) * width].astype(BF16) for f in range(folds)], axis=0
        )
        out_ref[part] = dot(spread_ref[...], stacked).astype(BF16)


def row_scan(x, columns, folds, gain, w_u, w_bc, rate, skip):
    parts, block, width = x.shape
    items = block // columns
    inner = w_u.shape[1]
    state = rate.shape[0]
    rows = parts * block
    w_b, w_c = w_bc[:, :state], w_bc[:, state:2 * state]
    w_b = jnp.concatenate([w_b, w_b], axis=1)
    w_c = jnp.concatenate([w_c, w_c], axis=1)
    return pl.pallas_call(
        functools.partial(row_kernel, parts, items, columns),
        name="row_scan",
        out_shape=jax.ShapeDtypeStruct((parts, folds * block, inner // folds), BF16),
        in_specs=[VMEM] * 9,
        out_specs=VMEM,
        scratch_shapes=[
            pltpu.VMEM((rows, width), BF16),
            pltpu.VMEM((rows, 2 * state), F32),
            pltpu.VMEM((rows, 2 * state), F32),
            pltpu.VMEM((rows, inner), F32),
            pltpu.VMEM((rows, inner), F32),
            pltpu.VMEM((rows * (parts * columns + 1) // 2, 2 * state), BF16),
        ],
        compiler_params=params(),
        cost_estimate=pl.CostEstimate(
            flops=2 * rows * width * inner * 16, bytes_accessed=4 << 20, transcendentals=0
        ),
    )(x, gain[None, :], w_u, w_b, w_c, rate, skip[None, :], row_order(items, columns),
      spread_order(items, folds, columns))


def home_kernel(folds, columns, x_ref, gain_ref, wz_ref, wm_ref, repeat_ref, gate_ref, mix_ref):
    block = repeat_ref.shape[1]
    tall = repeat_ref.shape[0]
    width = wz_ref.shape[1] // folds
    fold_of = (lax.broadcasted_iota(jnp.int32, (tall, 1), 0) % (folds * columns)) // columns
    for start in range(x_ref.shape[0] // block):
        here = normalise(x_ref[start * block:(start + 1) * block, :], gain_ref[...])
        here = dot(repeat_ref[...], here).astype(BF16)
        there = slice(start * tall, (start + 1) * tall)
        project = dot(here, wz_ref[...])
        gate = project[:, :width]
        for fold in range(1, folds):
            gate = jnp.where(fold_of == fold, project[:, fold * width:(fold + 1) * width], gate)
        gate = gate.astype(BF16).astype(F32)
        gate_ref[there, :] = gate / (1.0 + jnp.exp(-gate))
        mix_ref[there, :] = dot(here, wm_ref[...]).astype(BF16)


def home(x, items, columns, folds, gain, w_z, w_m):
    rows = x.shape[0]
    return pl.pallas_call(
        functools.partial(home_kernel, folds, columns),
        name="home",
        out_shape=(
            jax.ShapeDtypeStruct((rows * folds, w_z.shape[1] // folds), F32),
            jax.ShapeDtypeStruct((rows * folds, w_m.shape[1]), BF16),
        ),
        in_specs=[VMEM] * 5,
        out_specs=(VMEM, VMEM),
        compiler_params=params(),
        cost_estimate=pl.CostEstimate(
            flops=4 * rows * x.shape[1] * w_z.shape[1], bytes_accessed=4 << 20, transcendentals=0
        ),
    )(x, gain[None, :], w_z, w_m, repeat_order(items, folds, columns))


def col_kernel(state, y_ref, mix_ref, rate_ref, table_ref, out_ref, end_ref, held, decay, b_scr, c_scr, v_scr):
    width = y_ref.shape[1]
    step_count = y_ref.shape[0] // 8

    @pl.when(pl.program_id(0) == 0)
    def _():
        held[...] = jnp.zeros_like(held)
        decay[...] = jnp.exp(-rate_ref[...])

    b_scr[...] = dot(mix_ref[:, :state], table_ref[...])
    c_scr[...] = dot(mix_ref[:, state:], table_ref[...])
    v_scr[...] = y_ref[...].astype(F32)
    tiles = 2
    for first in range(0, width // LANES, tiles):
        spans = [slice((first + k) * LANES, (first + k + 1) * LANES) for k in range(tiles)]

        def step(t, carry):
            at = pl.ds(pl.multiple_of(t * 8, 8), 8)
            value = [v_scr[at, span] for span in spans]
            total = list(value)
            new = []
            for n in range(state):
                b = b_scr[at, n * LANES:(n + 1) * LANES]
                c = c_scr[at, n * LANES:(n + 1) * LANES]
                for k, span in enumerate(spans):
                    h = decay[n, :, span] * carry[n * tiles + k] + b * value[k]
                    total[k] = total[k] + c * h
                    new.append(h)
            for k, span in enumerate(spans):
                out_ref[at, span] = total[k]
            return tuple(new)

        start = tuple(held[n, :, span] for n in range(state) for span in spans)
        end = lax.fori_loop(0, step_count, step, start, unroll=2)
        for n in range(state):
            for k, span in enumerate(spans):
                held[n, :, span] = end[n * tiles + k]

    @pl.when(pl.program_id(0) == pl.num_programs(0) - 1)
    def _():
        end_ref[...] = held[...].astype(BF16)


def col_scan(y, mix, rate, steps_at_once):
    rows, width = y.shape
    state = rate.shape[0]
    block = steps_at_once * 8
    return pl.pallas_call(
        functools.partial(col_kernel, state),
        name="col_scan",
        grid=(rows // block,),
        out_shape=(
            jax.ShapeDtypeStruct((rows, width), F32),
            jax.ShapeDtypeStruct(rate.shape, BF16),
        ),
        in_specs=[
            pl.BlockSpec((block, width), lambda i: (i, 0)),
            pl.BlockSpec((block, 2 * state), lambda i: (i, 0)),
            pl.BlockSpec(rate.shape, lambda i: (0, 0, 0)),
            pl.BlockSpec((state, state * LANES), lambda i: (0, 0)),
        ],
        out_specs=(
            pl.BlockSpec((block, width), lambda i: (i, 0)),
            pl.BlockSpec(rate.shape, lambda i: (0, 0, 0)),
        ),
        scratch_shapes=[
            pltpu.VMEM(rate.shape, F32),
            pltpu.VMEM(rate.shape, F32),
            pltpu.VMEM((block, state * LANES), F32),
            pltpu.VMEM((block, state * LANES), F32),
            pltpu.VMEM((block, width), F32),
        ],
        compiler_params=params(),
        cost_estimate=pl.CostEstimate(flops=rows * width * 16 * 100, bytes_accessed=8 << 20, transcendentals=0),
    )(y, mix, rate, lane_table(state))


def last_kernel(state, folds, y_ref, gate_ref, mix_ref, in_ref, rate_ref, table_ref, order_ref, w_ref,
                out_ref, held, decay, c_scr, g_scr):
    width = y_ref.shape[1]
    step_count = y_ref.shape[0] // 8

    @pl.when(pl.program_id(0) == 0)
    def _():
        held[...] = in_ref[...].astype(F32)
        decay[...] = jnp.exp(-rate_ref[...])

    c_scr[...] = dot(mix_ref[:, state:], table_ref[...])
    tiles = 2
    for first in range(0, width // LANES, tiles):
        spans = [slice((first + k) * LANES, (first + k + 1) * LANES) for k in range(tiles)]

        def step(t, carry):
            at = pl.ds(pl.multiple_of(t * 8, 8), 8)
            total = [y_ref[at, span] for span in spans]
            new = []
            for n in range(state):
                c = c_scr[at, n * LANES:(n + 1) * LANES]
                for k, span in enumerate(spans):
                    h = decay[n, :, span] * carry[n * tiles + k]
                    total[k] = total[k] + c * h
                    new.append(h)
            for k, span in enumerate(spans):
                g_scr[at, span] = total[k] * gate_ref[at, span]
            return tuple(new)

        start = tuple(held[n, :, span] for n in range(state) for span in spans)
        end = lax.fori_loop(0, step_count, step, start, unroll=2)
        for n in range(state):
            for k, span in enumerate(spans):
                held[n, :, span] = end[n * tiles + k]

    gated = dot(order_ref[...], g_scr[...].astype(BF16)).astype(BF16)
    rows = gated.shape[0] // folds
    total = dot(gated[:rows], w_ref[:width, :])
    for fold in range(1, folds):
        total = total + dot(gated[fold * rows:(fold + 1) * rows], w_ref[fold * width:(fold + 1) * width, :])
    out_ref[...] = total.astype(BF16)


def last(y, gate, mix, incoming, rate, w_out, folds, columns, steps_at_once):
    rows, width = y.shape
    state = rate.shape[0]
    block = steps_at_once * 8
    return pl.pallas_call(
        functools.partial(last_kernel, state, folds),
        name="last",
        grid=(rows // block,),
        out_shape=jax.ShapeDtypeStruct((rows // folds, w_out.shape[1]), BF16),
        in_specs=[
            pl.BlockSpec((block, width), lambda i: (i, 0)),
            pl.BlockSpec((block, width), lambda i: (i, 0)),
            pl.BlockSpec((block, 2 * state), lambda i: (i, 0)),
            pl.BlockSpec(rate.shape, lambda i: (0, 0, 0)),
            pl.BlockSpec(rate.shape, lambda i: (0, 0, 0)),
            pl.BlockSpec((state, state * LANES), lambda i: (0, 0)),
            pl.BlockSpec((block, block), lambda i: (0, 0)),
            pl.BlockSpec(w_out.shape, lambda i: (0, 0)),
        ],
        out_specs=pl.BlockSpec((block // folds, w_out.shape[1]), lambda i: (i, 0)),
        scratch_shapes=[
            pltpu.VMEM(rate.shape, F32),
            pltpu.VMEM(rate.shape, F32),
            pltpu.VMEM((block, state * LANES), F32),
            pltpu.VMEM((block, width), F32),
        ],
        compiler_params=params(),
        cost_estimate=pl.CostEstimate(flops=rows * width * 16 * 60, bytes_accessed=8 << 20, transcendentals=0),
    )(y, gate, mix, incoming, rate, lane_table(state), gather_order(steps_at_once, folds, columns), w_out)


def wide_row_scan(x, columns, folds, gain, w_u, w_bc, rate, skip):
    parts, block, width = x.shape
    items = block // columns
    inner = w_u.shape[1]
    state = rate.shape[0]
    normed = normalise(x.reshape(parts, items, columns, width), gain)
    normed = normed.transpose(0, 2, 1, 3).reshape(parts * columns, items, width)
    value = dot(normed, w_u).astype(BF16).astype(F32)
    mix = dot(normed, w_bc).astype(BF16).astype(F32)
    factor = jnp.exp(-rate)

    def advance(held, now):
        value_now, inject, readout = now
        held = factor * held + inject[:, :, None] * value_now[:, None, :]
        return held, jnp.sum(held * readout[:, :, None], axis=1) + skip * value_now

    start = jnp.zeros((items, state, inner), F32)
    _, out = lax.scan(advance, start, (value, mix[..., :state], mix[..., state:2 * state]))
    out = out.astype(BF16).reshape(parts, columns, items, folds, inner // folds)
    return out.transpose(0, 2, 3, 1, 4).reshape(parts, folds * block, inner // folds)


def per_device(tokens, norm_gain, w_in, w_bc, rate_row, rate_col, skip_gain, w_out):
    height, columns, features = tokens.shape
    inner = w_out.shape[0]
    state = rate_row.shape[0]
    parts = lax.axis_size("rows")
    items = height // parts
    folds = 8 // columns
    steps_at_once = 16
    tokens = tokens.reshape(height * columns, features)
    moved = lax.all_to_all(
        tokens.reshape(parts, items * columns, features), "rows", split_axis=0, concat_axis=0, tiled=True
    )
    gate, mix = home(tokens, steps_at_once, columns, folds, norm_gain, w_in[:, inner:], w_bc[:, 2 * state:])
    scan = row_scan if items % 8 == 0 and parts * columns <= 64 else wide_row_scan
    row_mixed = scan(
        moved, columns, folds, norm_gain, w_in[:, :inner], w_bc[:, :2 * state], rate_row, skip_gain
    )
    back = lax.all_to_all(row_mixed, "rows", split_axis=0, concat_axis=0, tiled=True)
    back = back.reshape(height * folds * columns, inner // folds)
    rate = jnp.repeat(rate_col.reshape(state, folds, inner // folds), columns, axis=1)
    col, end = col_scan(back, mix, rate, steps_at_once)
    size, here = lax.axis_size("cols"), lax.axis_index("cols")
    incoming = jnp.zeros_like(end)
    for k in range(size - 1):
        if k == 0:
            carried = end
        else:
            carried = (jnp.exp(-rate * height) * incoming.astype(F32) + end.astype(F32)).astype(BF16)
        arrived = lax.ppermute(carried, "cols", [(k, k + 1)])
        incoming = arrived if k == 0 else jnp.where(here == k + 1, arrived, incoming)
    out = last(col, gate, mix, incoming, rate, w_out, folds, columns, steps_at_once)
    return out.reshape(height, columns, features)


def solution(mesh):
    placed = (P(("slides", "cols"), "rows", None), P(), P(), P(), P(), P(), P(), P())
    return jax.shard_map(
        per_device,
        mesh=mesh,
        in_specs=placed,
        out_specs=P(("slides", "cols"), "rows", None),
        check_vma=False,
    )
```

```python
import functools

import jax
import jax.numpy as jnp
import numpy as np
from jax import lax
from jax.experimental import pallas as pl
from jax.experimental.pallas import tpu as pltpu
from jax.sharding import PartitionSpec as P

F32 = jnp.float32
BF16 = jnp.bfloat16
VMEM = pl.BlockSpec(memory_space=pltpu.VMEM)
LANES = 128


def normalise(tokens, gain):
    as_float = tokens.astype(F32)
    scale_now = lax.rsqrt(jnp.mean(as_float * as_float, axis=-1, keepdims=True) + 1e-05)
    return (as_float * scale_now * gain).astype(BF16)


def dot(a, b):
    return jnp.dot(a, b, preferred_element_type=F32)


def params():
    return pltpu.CompilerParams(vmem_limit_bytes=40 << 20)


def selection(shape, sources):
    matrix = np.zeros(shape, np.float32)
    matrix[np.arange(shape[0]), sources] = 1.0
    return jnp.asarray(matrix, BF16)


def row_order(items, columns):
    c, i = np.divmod(np.arange(items * columns), items)
    return selection((items * columns,) * 2, i * columns + c)


def spread_order(items, folds, columns):
    i, rest = np.divmod(np.arange(items * folds * columns), folds * columns)
    return selection((items * folds * columns,) * 2, rest * items + i)


def repeat_order(items, folds, columns):
    i, rest = np.divmod(np.arange(items * folds * columns), folds * columns)
    return selection((items * folds * columns, items * columns), i * columns + rest % columns)


def gather_order(items, folds, columns):
    f, rest = np.divmod(np.arange(items * folds * columns), items * columns)
    i, c = np.divmod(rest, columns)
    return selection((items * folds * columns,) * 2, (i * folds + f) * columns + c)


def lane_table(state):
    return jnp.asarray(np.repeat(np.eye(state, dtype=np.float32), LANES, axis=1), BF16)


def row_kernel(parts, items, columns, x_ref, gain_ref, wu_ref, wb_ref, wc_ref, rate_ref, skip_ref,
               order_ref, spread_ref, out_ref, normed, b_scr, c_scr, u_scr, y_scr, g_scr):
    block = items * columns
    steps = parts * columns
    rows = steps * items
    inner = u_scr.shape[1]
    folds = spread_ref.shape[0] // block
    gain = gain_ref[...]
    for part in range(parts):
        here = normalise(x_ref[part], gain)
        normed[part * block:(part + 1) * block, :] = dot(order_ref[...], here).astype(BF16)
    b_scr[...] = dot(normed[...], wb_ref[...]).astype(BF16).astype(F32)
    c_scr[...] = dot(normed[...], wc_ref[...]).astype(BF16).astype(F32)
    chunk = 128
    pieces = []
    at = 0
    for lag in range(steps):
        first = lag * items
        while first < rows:
            count = min(chunk, rows - first)
            pieces.append((lag, first, count, at))
            first += count
            at += count
    for lag, first, count, at in pieces:
        source = first - lag * items
        product = c_scr[first:first + count, :] * b_scr[source:source + count, :]
        g_scr[at:at + count, :] = product.astype(BF16)
    tile = 512

    def one_tile(tile_id, _):
        where = pl.ds(pl.multiple_of(tile_id * tile, tile), tile)
        u_scr[:, where] = dot(normed[...], wu_ref[:, where]).astype(BF16).astype(F32)
        rate = rate_ref[:, where]
        skip = skip_ref[:, where]
        done = -1
        table = None
        for lag, first, count, at in pieces:
            if lag != done:
                power = jnp.exp(rate * (-float(lag)))
                high = power.astype(BF16)
                low = (power - high.astype(F32)).astype(BF16)
                table = jnp.concatenate([high, low], axis=0)
                done = lag
            matrix = dot(g_scr[at:at + count, :], table)
            source = first - lag * items
            value = u_scr[source:source + count, where]
            if lag == 0:
                y_scr[first:first + count, where] = (matrix + skip) * value
            else:
                y_scr[first:first + count, where] += matrix * value
        return 0

    lax.fori_loop(0, inner // tile, one_tile, 0)
    width = out_ref.shape[2]
    halves = out_ref.shape[0] // parts
    for part in range(parts):
        here = slice(part * block, (part + 1) * block)
        for half in range(halves):
            first = half * folds * width
            stacked = jnp.concatenate(
                [y_scr[here, first + f * width:first + (f + 1) * width].astype(BF16) for f in range(folds)], axis=0
            )
            out_ref[part * halves + half] = dot(spread_ref[...], stacked).astype(BF16)


def row_scan(x, columns, folds, halves, gain, w_u, w_bc, rate, skip):
    parts, block, width = x.shape
    items = block // columns
    inner = w_u.shape[1]
    state = rate.shape[0]
    rows = parts * block
    w_b, w_c = w_bc[:, :state], w_bc[:, state:2 * state]
    w_b = jnp.concatenate([w_b, w_b], axis=1)
    w_c = jnp.concatenate([w_c, w_c], axis=1)
    return pl.pallas_call(
        functools.partial(row_kernel, parts, items, columns),
        name="row_scan",
        out_shape=jax.ShapeDtypeStruct((parts * halves, folds * block, inner // (halves * folds)), BF16),
        in_specs=[VMEM] * 9,
        out_specs=VMEM,
        scratch_shapes=[
            pltpu.VMEM((rows, width), BF16),
            pltpu.VMEM((rows, 2 * state), F32),
            pltpu.VMEM((rows, 2 * state), F32),
            pltpu.VMEM((rows, inner), F32),
            pltpu.VMEM((rows, inner), F32),
            pltpu.VMEM((rows * (parts * columns + 1) // 2, 2 * state), BF16),
        ],
        compiler_params=params(),
        cost_estimate=pl.CostEstimate(
            flops=2 * rows * width * inner * 16, bytes_accessed=4 << 20, transcendentals=0
        ),
    )(x, gain[None, :], w_u, w_b, w_c, rate, skip[None, :], row_order(items, columns),
      spread_order(items, folds, columns))


def home_kernel(folds, columns, x_ref, gain_ref, wz_ref, wm_ref, repeat_ref, gate_ref, mix_ref):
    block = repeat_ref.shape[1]
    tall = repeat_ref.shape[0]
    width = wz_ref.shape[1] // folds
    fold_of = (lax.broadcasted_iota(jnp.int32, (tall, 1), 0) % (folds * columns)) // columns
    for start in range(x_ref.shape[0] // block):
        here = normalise(x_ref[start * block:(start + 1) * block, :], gain_ref[...])
        here = dot(repeat_ref[...], here).astype(BF16)
        there = slice(start * tall, (start + 1) * tall)
        project = dot(here, wz_ref[...])
        gate = project[:, :width]
        for fold in range(1, folds):
            gate = jnp.where(fold_of == fold, project[:, fold * width:(fold + 1) * width], gate)
        gate = gate.astype(BF16).astype(F32)
        gate_ref[there, :] = gate / (1.0 + jnp.exp(-gate))
        mix_ref[there, :] = dot(here, wm_ref[...]).astype(BF16)


def home(x, items, columns, folds, gain, w_z, w_m):
    rows = x.shape[0]
    return pl.pallas_call(
        functools.partial(home_kernel, folds, columns),
        name="home",
        out_shape=(
            jax.ShapeDtypeStruct((rows * folds, w_z.shape[1] // folds), F32),
            jax.ShapeDtypeStruct((rows * folds, w_m.shape[1]), BF16),
        ),
        in_specs=[VMEM] * 5,
        out_specs=(VMEM, VMEM),
        compiler_params=params(),
        cost_estimate=pl.CostEstimate(
            flops=4 * rows * x.shape[1] * w_z.shape[1], bytes_accessed=4 << 20, transcendentals=0
        ),
    )(x, gain[None, :], w_z, w_m, repeat_order(items, folds, columns))


def col_kernel(state, halves, core_ref, y_ref, gate_ref, mix_ref, next_ref, rate_ref, table_ref, *rest):
    outs, (held, decay, b0, c0, b1, c1, v_scr, g_scr) = rest[:halves], rest[halves:]
    block = b0.shape[0]
    steps = block // 8
    width = held.shape[2]
    tiles = width // LANES
    spans = [slice(k * LANES, (k + 1) * LANES) for k in range(tiles)]
    per_tile = 2 * LANES
    pieces = [(w, p) for p in range(state * LANES // per_tile) for w in range(2)]

    def spread(rows, which, piece, targets):
        there = slice(piece * per_tile, (piece + 1) * per_tile)
        targets[which][:, there] = dot(rows[:, which * state:(which + 1) * state], table_ref[:, there])

    @pl.when(pl.program_id(0) == 0)
    def _():
        held[...] = jnp.zeros_like(held)
        decay[...] = jnp.exp(-rate_ref[...])
        for which, piece in pieces:
            spread(mix_ref[0, :block, :], which, piece, (b0, c0))

    source_rows = y_ref.shape[2]
    for k in range(y_ref.shape[0]):
        v_scr[k * source_rows:(k + 1) * source_rows, :] = y_ref[k, 0].astype(F32)

    def scan(offset, b_scr, c_scr, ahead, targets):
        carry = [held[n, :, span] for n in range(state) for span in spans]
        done = 0
        for t in range(steps):
            while done < len(pieces) * (t + 1) // steps:
                spread(ahead, *pieces[done], targets)
                done += 1
            here = slice(t * 8, t * 8 + 8)
            rows = slice(offset + t * 8, offset + t * 8 + 8)
            value = [v_scr[rows, span] for span in spans]
            total = list(value)
            for n in range(state):
                b = b_scr[here, n * LANES:(n + 1) * LANES]
                c = c_scr[here, n * LANES:(n + 1) * LANES]
                for k, span in enumerate(spans):
                    h = decay[n, :, span] * carry[n * tiles + k] + b * value[k]
                    total[k] = total[k] + c * h
                    carry[n * tiles + k] = h
            for k, span in enumerate(spans):
                g_scr[rows, span] = total[k] * gate_ref[0, rows, span]
        for n in range(state):
            for k, span in enumerate(spans):
                held[n, :, span] = carry[n * tiles + k]

    scan(0, b0, c0, mix_ref[0, block:, :], (b1, c1))
    scan(block, b1, c1, next_ref[0, :block, :], (b0, c0))
    per_half = pl.num_programs(0) // halves
    slot = lax.rem(pl.program_id(0) // per_half + halves - core_ref[0], halves)
    for s in range(halves):
        @pl.when(slot == s)
        def _(s=s):
            outs[s][...] = g_scr[...].astype(BF16)


def col_scan(core, y, gate, mix, rate):
    sources, halves, source_rows, width = y.shape
    state = rate.shape[0]
    take = max(1, min(sources, 256 // source_rows))
    block = take * source_rows
    per_half = sources // take
    last_step = halves * per_half - 1

    def slot(i, core):
        return lax.rem(i // per_half + halves - core[0], halves)

    def out_map(s):
        def place(i, core):
            first = lax.rem(core[0] + s, halves) * per_half
            return (jnp.clip(i - first, 0, per_half - 1), 0)
        return place

    half_block = block // 2
    return pl.pallas_call(
        functools.partial(col_kernel, state, halves),
        name="col_scan",
        grid_spec=pltpu.PrefetchScalarGridSpec(
            num_scalar_prefetch=1,
            grid=(halves * per_half,),
            in_specs=[
                pl.BlockSpec((take, 1, source_rows, width), lambda i, core: (i % per_half, i // per_half, 0, 0)),
                pl.BlockSpec((1, block, width), lambda i, core: (slot(i, core), i % per_half, 0)),
                pl.BlockSpec((1, block, 2 * state), lambda i, core: (slot(i, core), i % per_half, 0)),
                pl.BlockSpec((1, block, 2 * state), lambda i, core: (
                    slot(jnp.minimum(i + 1, last_step), core), jnp.minimum(i + 1, last_step) % per_half, 0)),
                pl.BlockSpec(rate.shape, lambda i, core: (0, 0, 0)),
                pl.BlockSpec((state, state * LANES), lambda i, core: (0, 0)),
            ],
            out_specs=[pl.BlockSpec((block, width), out_map(s)) for s in range(halves)],
            scratch_shapes=[
                pltpu.VMEM(rate.shape, F32),
                pltpu.VMEM(rate.shape, F32),
                pltpu.VMEM((half_block, state * LANES), F32),
                pltpu.VMEM((half_block, state * LANES), F32),
                pltpu.VMEM((half_block, state * LANES), F32),
                pltpu.VMEM((half_block, state * LANES), F32),
                pltpu.VMEM((block, width), F32),
                pltpu.VMEM((block, width), F32),
            ],
        ),
        out_shape=[jax.ShapeDtypeStruct((per_half * block, width), BF16)] * halves,
        compiler_params=params(),
        cost_estimate=pl.CostEstimate(flops=5 * halves * per_half * block * width * state, bytes_accessed=8 << 20,
                                      transcendentals=0),
    )(core, y, gate, mix, mix, rate, lane_table(state))


def last_kernel(folds, halves, *refs):
    parts, (order_ref, w_ref, out_ref) = refs[:halves], refs[halves:]
    block = order_ref.shape[0]
    rows = block // folds
    width = parts[0].shape[1]
    for at in range(parts[0].shape[0] // block):
        here = slice(at * block, (at + 1) * block)
        gated = jnp.concatenate([part[here, :] for part in parts], axis=1)
        gated = dot(order_ref[...], gated).astype(BF16)
        total = dot(gated[:rows], w_ref[0])
        for fold in range(1, folds):
            total = total + dot(gated[fold * rows:(fold + 1) * rows], w_ref[fold])
        out_ref[at * rows:(at + 1) * rows, :] = total.astype(BF16)


def last(parts, w_out, items, folds, columns):
    rows = parts[0].shape[0] // folds
    features = w_out.shape[2]
    return pl.pallas_call(
        functools.partial(last_kernel, folds, len(parts)),
        name="last",
        out_shape=jax.ShapeDtypeStruct((rows, features), BF16),
        in_specs=[VMEM] * (len(parts) + 2),
        out_specs=VMEM,
        compiler_params=params(),
        cost_estimate=pl.CostEstimate(flops=2 * rows * w_out.size // folds, bytes_accessed=2 << 20, transcendentals=0),
    )(*parts, gather_order(items, folds, columns), w_out)


def wide_row_scan(x, columns, folds, halves, gain, w_u, w_bc, rate, skip):
    parts, block, width = x.shape
    items = block // columns
    inner = w_u.shape[1]
    state = rate.shape[0]
    normed = normalise(x.reshape(parts, items, columns, width), gain)
    normed = normed.transpose(0, 2, 1, 3).reshape(parts * columns, items, width)
    value = dot(normed, w_u).astype(BF16).astype(F32)
    mix = dot(normed, w_bc).astype(BF16).astype(F32)
    factor = jnp.exp(-rate)

    def advance(held, now):
        value_now, inject, readout = now
        held = factor * held + inject[:, :, None] * value_now[:, None, :]
        return held, jnp.sum(held * readout[:, :, None], axis=1) + skip * value_now

    start = jnp.zeros((items, state, inner), F32)
    _, out = lax.scan(advance, start, (value, mix[..., :state], mix[..., state:2 * state]))
    narrow = inner // (halves * folds)
    out = out.astype(BF16).reshape(parts, columns, items, halves, folds, narrow)
    return out.transpose(0, 3, 2, 4, 1, 5).reshape(parts * halves, folds * block, narrow)


def per_device(tokens, norm_gain, w_in, w_bc, rate_row, rate_col, skip_gain, w_out):
    height, columns, features = tokens.shape
    inner = w_out.shape[0]
    state = rate_row.shape[0]
    parts, halves = lax.axis_size("rows"), lax.axis_size("cols")
    core = lax.axis_index("cols")
    both = ("rows", "cols")
    sources = parts * halves
    items = height // sources
    folds = 8 // columns
    group = inner // halves
    width = group // folds
    tokens = tokens.reshape(height * columns, features)
    moved = lax.all_to_all(
        tokens.reshape(sources, items * columns, features), both, split_axis=0, concat_axis=0, tiled=True
    )
    scan = row_scan if items * halves % 8 == 0 and parts * columns <= 64 else wide_row_scan
    row_mixed = scan(
        moved.reshape(parts, halves * items * columns, features), columns, folds, halves, norm_gain,
        w_in[:, :inner], w_bc[:, :2 * state], rate_row, skip_gain
    )
    back = lax.all_to_all(row_mixed, both, split_axis=0, concat_axis=0, tiled=True)

    whole = [tokens] + [
        lax.ppermute(tokens, "cols", [(k, (k - s) % halves) for k in range(halves)]) for s in range(1, halves)
    ]
    own = core * group
    w_gate = lax.dynamic_slice_in_dim(w_in, inner + own, group, 1)
    pieces = [home(t, 16, columns, folds, norm_gain, w_gate, w_bc[:, 2 * state:]) for t in whole]
    gate = jnp.stack([piece[0] for piece in pieces])
    mix = jnp.stack([piece[1] for piece in pieces])
    rate = lax.dynamic_slice_in_dim(rate_col, own, group, 1)
    rate = jnp.repeat(rate.reshape(state, folds, width), columns, axis=1)
    back = back.reshape(sources, halves, items * folds * columns, width)
    if items * folds * columns % 16 != 0:
        blocks = max(1, height * folds * columns // 256)
        back = back.reshape(blocks, sources // blocks, halves, -1, width).transpose(0, 2, 1, 3, 4)
        back = back.reshape(blocks, halves, -1, width)
    gated = col_scan(core.reshape(1), back, gate, mix, rate)
    groups = [gated[0]] + [
        lax.ppermute(gated[s], "cols", [(k, (k + s) % halves) for k in range(halves)]) for s in range(1, halves)
    ]
    w_out = w_out.reshape(halves, folds, width, features)
    w_last = jnp.stack([w_out[(core - s) % halves] for s in range(halves)], axis=1)
    w_last = w_last.reshape(folds, halves * width, features)
    return last(groups, w_last, 16, folds, columns).reshape(height, columns, features)


def solution(mesh):
    placed = (P(("slides", "cols"), "rows", None), P(), P(), P(), P(), P(), P(), P())
    return jax.shard_map(
        per_device,
        mesh=mesh,
        in_specs=placed,
        out_specs=P(("slides", "cols"), "rows", None),
        check_vma=False,
    )
```

```python
import functools

import jax
import jax.numpy as jnp
import numpy as np
from jax import lax
from jax.experimental import pallas as pl
from jax.experimental.pallas import tpu as pltpu
from jax.sharding import PartitionSpec as P

F32 = jnp.float32
BF16 = jnp.bfloat16
VMEM = pl.BlockSpec(memory_space=pltpu.VMEM)
LANES = 128
AHEAD = 3


def normalise(tokens, gain):
    as_float = tokens.astype(F32)
    scale_now = lax.rsqrt(jnp.mean(as_float * as_float, axis=-1, keepdims=True) + 1e-05)
    return (as_float * scale_now * gain).astype(BF16)


def dot(a, b):
    return jnp.dot(a, b, preferred_element_type=F32)


def params(mebibytes):
    return pltpu.CompilerParams(vmem_limit_bytes=mebibytes << 20)


def selection(shape, sources):
    matrix = np.zeros(shape, np.float32)
    matrix[np.arange(shape[0]), sources] = 1.0
    return jnp.asarray(matrix, BF16)


def row_order(items, columns):
    c, i = np.divmod(np.arange(items * columns), items)
    return selection((items * columns,) * 2, i * columns + c)


def lane_order(columns):
    part, rest = np.divmod(np.arange(columns * LANES), LANES)
    column, channel = np.divmod(rest, LANES // columns)
    return selection((columns * LANES,) * 2, column * LANES + part * (LANES // columns) + channel).T


def lane_table(columns, count):
    lane = np.arange(count * LANES)
    matrix = np.zeros((columns, count, count * LANES), np.float32)
    matrix[lane % LANES // (LANES // columns), lane // LANES, lane] = 1.0
    return jnp.asarray(matrix, BF16)


def row_kernel(parts, items, columns, x_ref, gain_ref, wu_ref, wb_ref, wc_ref, rate_ref, skip_ref,
               order_ref, lane_ref, out_ref, normed, b_scr, c_scr, u_scr, y_scr, g_scr, l_scr):
    block = items * columns
    steps = parts * columns
    rows = steps * items
    inner = u_scr.shape[1]
    gain = gain_ref[...]
    for part in range(parts):
        here = normalise(x_ref[part], gain)
        normed[part * block:(part + 1) * block, :] = dot(order_ref[...], here).astype(BF16)
    b_scr[...] = dot(normed[...], wb_ref[...]).astype(BF16).astype(F32)
    c_scr[...] = dot(normed[...], wc_ref[...]).astype(BF16).astype(F32)
    chunk = 128
    pieces = []
    at = 0
    for lag in range(steps):
        first = lag * items
        while first < rows:
            count = min(chunk, rows - first)
            pieces.append((lag, first, count, at))
            first += count
            at += count
    for lag, first, count, at in pieces:
        source = first - lag * items
        product = c_scr[first:first + count, :] * b_scr[source:source + count, :]
        g_scr[at:at + count, :] = product.astype(BF16)
    tile = 512

    def one_tile(tile_id, _):
        where = pl.ds(pl.multiple_of(tile_id * tile, tile), tile)
        u_scr[:, where] = dot(normed[...], wu_ref[:, where]).astype(BF16).astype(F32)
        rate = rate_ref[:, where]
        skip = skip_ref[:, where]
        done = -1
        table = None
        for lag, first, count, at in pieces:
            if lag != done:
                power = jnp.exp(rate * (-float(lag)))
                high = power.astype(BF16)
                low = (power - high.astype(F32)).astype(BF16)
                table = jnp.concatenate([high, low], axis=0)
                done = lag
            matrix = dot(g_scr[at:at + count, :], table)
            source = first - lag * items
            value = u_scr[source:source + count, where]
            if lag == 0:
                y_scr[first:first + count, where] = (matrix + skip) * value
            else:
                y_scr[first:first + count, where] += matrix * value
        return 0

    lax.fori_loop(0, inner // tile, one_tile, 0)
    for part in range(parts):
        for column in range(columns):
            here = slice((part * columns + column) * items, (part * columns + column + 1) * items)
            for at in range(inner // LANES):
                there = slice((at * columns + column) * LANES, (at * columns + column + 1) * LANES)
                l_scr[part * items:(part + 1) * items, there] = y_scr[here, at * LANES:(at + 1) * LANES].astype(BF16)
    halves = out_ref.shape[0] // parts
    few = items // halves
    groups = out_ref.shape[2] // few
    for at in range(inner // LANES):
        span = columns * LANES
        turned = dot(l_scr[:, at * span:(at + 1) * span], lane_ref[...])
        half, first = divmod(at * columns, groups)
        for part in range(parts):
            for own in range(halves):
                rows_at = part * items + own * few
                for k in range(0, columns, 2):
                    pair = jnp.concatenate(
                        [turned[rows_at:rows_at + few, (k + j) * LANES:(k + j + 1) * LANES] for j in range(2)], axis=0
                    )
                    out_ref[part * halves + half, own, (first + k) * few:(first + k + 2) * few, :] = pair.astype(BF16)


def row_scan(x, columns, halves, gain, w_u, w_bc, rate, skip):
    parts, block, width = x.shape
    items = block // columns
    inner = w_u.shape[1]
    state = rate.shape[0]
    rows = parts * block
    w_b, w_c = w_bc[:, :state], w_bc[:, state:2 * state]
    w_b = jnp.concatenate([w_b, w_b], axis=1)
    w_c = jnp.concatenate([w_c, w_c], axis=1)
    return pl.pallas_call(
        functools.partial(row_kernel, parts, items, columns),
        name="row_scan",
        out_shape=jax.ShapeDtypeStruct(
            (parts * halves, halves, inner * columns // (halves * LANES) * (items // halves), LANES), BF16
        ),
        in_specs=[VMEM] * 9,
        out_specs=VMEM,
        scratch_shapes=[
            pltpu.VMEM((rows, width), BF16),
            pltpu.VMEM((rows, 2 * state), F32),
            pltpu.VMEM((rows, 2 * state), F32),
            pltpu.VMEM((rows, inner), F32),
            pltpu.VMEM((rows, inner), F32),
            pltpu.VMEM((rows * (parts * columns + 1) // 2, 2 * state), BF16),
            pltpu.VMEM((parts * items, columns * inner), BF16),
        ],
        compiler_params=params(20),
        cost_estimate=pl.CostEstimate(
            flops=2 * rows * width * inner * 16, bytes_accessed=4 << 20, transcendentals=0
        ),
    )(x, gain[None, :], w_u, w_b, w_c, rate, skip[None, :], row_order(items, columns),
      lane_order(columns))


def home_kernel(columns, halves, gain_ref, wz_ref, wm_ref, order_ref, lane_ref, table_ref, *refs):
    x_refs, (gate_ref, mix_ref, n_scr) = refs[:halves], refs[halves:]
    block = order_ref.shape[0]
    items = block // columns
    steps = x_refs[0].shape[0] // columns
    groups = gate_ref.shape[1] // steps
    for half, x_ref in enumerate(x_refs):
        for start in range(x_ref.shape[0] // block):
            here = normalise(x_ref[start * block:(start + 1) * block, :], gain_ref[...])
            here = dot(order_ref[...], here).astype(BF16)
            for column in range(columns):
                first = column * steps + start * items
                n_scr[first:first + items, :] = here[column * items:(column + 1) * items]
        mix = None
        project = []
        for column in range(columns):
            here = n_scr[column * steps:(column + 1) * steps, :]
            project.append(dot(here, wz_ref[...]).astype(BF16))
            part = dot(dot(here, wm_ref[...]).astype(BF16), table_ref[column])
            mix = part if mix is None else mix + part
        for n in range(mix_ref.shape[2]):
            for at in range(steps // items):
                mix_ref[half, at, n] = mix[at * items:(at + 1) * items, n * LANES:(n + 1) * LANES]
        for at in range(wz_ref.shape[1] // LANES):
            joined = jnp.concatenate([part[:, at * LANES:(at + 1) * LANES] for part in project], axis=1)
            gate = dot(joined, lane_ref[...])
            gate = gate / (1.0 + jnp.exp(-gate))
            for k in range(columns):
                gate_ref[half, pl.ds(at * columns + k, steps, stride=groups), :] = gate[:, k * LANES:(k + 1) * LANES]


def home(tokens, items, columns, gain, w_z, w_m):
    halves = len(tokens)
    rows, width = tokens[0].shape
    steps = rows // columns
    groups = w_z.shape[1] * columns // LANES
    count = w_m.shape[1]
    gate, mix = pl.pallas_call(
        functools.partial(home_kernel, columns, halves),
        name="home",
        out_shape=(
            jax.ShapeDtypeStruct((halves, steps * groups, LANES), F32),
            jax.ShapeDtypeStruct((halves, steps // items, count, items, LANES), F32),
        ),
        in_specs=[VMEM] * (6 + halves),
        out_specs=(VMEM, VMEM),
        scratch_shapes=[pltpu.VMEM((rows, width), BF16)],
        compiler_params=params(20),
        cost_estimate=pl.CostEstimate(
            flops=4 * halves * rows * width * w_z.shape[1], bytes_accessed=8 << 20, transcendentals=0
        ),
    )(gain[None, :], w_z, w_m, row_order(items, columns), lane_order(columns), lane_table(columns, count), *tokens)
    return gate.reshape(halves, steps, groups, LANES), mix


def col_kernel(state, halves, core_ref, y_hbm, gate_hbm, mix_hbm, rate_hbm, *rest):
    outs = rest[:halves]
    y_ref, gate_ref, mix_ref, out_ref, held, decay, v_scr, g_scr, sems = rest[halves:]
    per_half, _, span_steps, _ = mix_hbm.shape[1:]
    count = halves * per_half
    groups = gate_hbm.shape[2]
    take = y_hbm.shape[0] // per_half
    items = span_steps // take
    tiles = groups // 8
    spans = [slice(f * 8, f * 8 + 8) for f in range(tiles)]

    def slot_of(at):
        return lax.rem(at // per_half + halves - core_ref[0], halves)

    def copies(at):
        half, place, slot = at // per_half, at % per_half, slot_of(at)
        first = pl.multiple_of(place * span_steps, span_steps)
        return (
            pltpu.make_async_copy(y_hbm.at[pl.ds(place * take, take), half], y_ref.at[at], sems.at[at, 0]),
            pltpu.make_async_copy(mix_hbm.at[slot, place], mix_ref.at[at], sems.at[at, 1]),
            pltpu.make_async_copy(gate_hbm.at[slot, pl.ds(first, span_steps)], gate_ref.at[at], sems.at[at, 2]),
        )

    def result(at, s):
        return pltpu.make_async_copy(out_ref.at[at], outs[s].at[at % per_half], sems.at[at, 3])

    def launch(at, _):
        for copy in copies(at):
            copy.start()
        return 0

    first_copy = pltpu.make_async_copy(rate_hbm, decay, sems.at[count, 0])
    first_copy.start()
    lax.fori_loop(0, min(AHEAD, count), launch, 0)
    held[...] = jnp.zeros_like(held)
    first_copy.wait()
    decay[...] = jnp.exp(-decay[...])

    def one_span(at, _):
        for copy in copies(at):
            copy.wait()

        @pl.when(at + AHEAD < count)
        def _():
            launch(at + AHEAD, 0)

        for k in range(take):
            v_scr[k * groups * items:(k + 1) * groups * items, :] = y_ref[at, k].astype(F32)
        carry = [held[n, span, :] for n in range(state) for span in spans]
        for t in range(span_steps):
            k, i = divmod(t, items)
            value = [v_scr[pl.ds((k * groups + f * 8) * items + i, 8, stride=items), :] for f in range(tiles)]
            total = list(value)
            for n in range(state):
                b = jnp.broadcast_to(mix_ref[at, n, t:t + 1, :], (8, LANES))
                c = jnp.broadcast_to(mix_ref[at, state + n, t:t + 1, :], (8, LANES))
                for f, span in enumerate(spans):
                    h = decay[n, span, :] * carry[n * tiles + f] + b * value[f]
                    total[f] = total[f] + c * h
                    carry[n * tiles + f] = h
            for f, span in enumerate(spans):
                g_scr[pl.ds(f * 8 * span_steps + t, 8, stride=span_steps), :] = total[f] * gate_ref[at, t, span, :]
        for n in range(state):
            for f, span in enumerate(spans):
                held[n, span, :] = carry[n * tiles + f]
        out_ref[at] = g_scr[...].astype(BF16)
        for s in range(halves):
            @pl.when(slot_of(at) == s)
            def _(s=s):
                result(at, s).start()
        return 0

    lax.fori_loop(0, count, one_span, 0)

    def finish(at, _):
        for s in range(halves):
            @pl.when(slot_of(at) == s)
            def _(s=s):
                result(at, s).wait()
        return 0

    lax.fori_loop(0, count, finish, 0)


def col_scan(core, y, gate, mix, rate):
    sources, halves, rows, _ = y.shape
    state, groups, _ = rate.shape
    per_half, _, span_steps, _ = mix.shape[1:]
    count = halves * per_half
    far = pl.BlockSpec(memory_space=pltpu.HBM)
    return pl.pallas_call(
        functools.partial(col_kernel, state, halves),
        name="col_scan",
        in_specs=[pl.BlockSpec(memory_space=pltpu.SMEM)] + [far] * 4,
        out_specs=[far] * halves,
        scratch_shapes=[
            pltpu.VMEM((count, sources // per_half, rows, LANES), BF16),
            pltpu.VMEM((count, span_steps, groups, LANES), F32),
            pltpu.VMEM((count, 2 * state, span_steps, LANES), F32),
            pltpu.VMEM((count, groups * span_steps, LANES), BF16),
            pltpu.VMEM(rate.shape, F32),
            pltpu.VMEM(rate.shape, F32),
            pltpu.VMEM((span_steps * groups, LANES), F32),
            pltpu.VMEM((span_steps * groups, LANES), F32),
            pltpu.SemaphoreType.DMA((count + 1, 4)),
        ],
        out_shape=[jax.ShapeDtypeStruct((per_half, groups * span_steps, LANES), BF16)] * halves,
        compiler_params=params(62),
        cost_estimate=pl.CostEstimate(flops=5 * count * span_steps * groups * LANES * state,
                                      bytes_accessed=8 << 20, transcendentals=0),
    )(core, y, gate, mix, rate)


def last_kernel(columns, halves, group_ref, part_ref, w_ref, lane_ref, *refs):
    out_ref, l_scr = refs[-2:]
    spans, rows, _ = part_ref.shape
    width = w_ref.shape[0] // halves
    groups = width * columns // LANES
    span = rows // groups
    steps = spans * span
    for at in range(width // LANES):
        joined = jnp.concatenate([
            jnp.concatenate([
                part_ref[p, (at * columns + k) * span:(at * columns + k + 1) * span, :] for p in range(spans)
            ], axis=0) for k in range(columns)
        ], axis=1)
        turned = dot(joined, lane_ref[...])
        for column in range(columns):
            l_scr[at, pl.ds(column, steps, stride=columns), :] = turned[:, column * LANES:(column + 1) * LANES]
    first = pl.multiple_of(group_ref[0] * width, width)
    gated = jnp.concatenate([l_scr[at].astype(BF16) for at in range(width // LANES)], axis=1)
    total = dot(gated, w_ref[pl.ds(first, width), :])
    if len(refs) > 2:
        total = total + refs[0][...]
    out_ref[...] = total.reshape(out_ref.shape).astype(out_ref.dtype)


def last(group, part, w_out, columns, halves, before, out_type):
    inner, features = w_out.shape
    groups = inner * columns // (halves * LANES)
    steps = part.shape[0] * part.shape[1] // groups
    rows = steps * columns
    others = () if before is None else (before,)
    return pl.pallas_call(
        functools.partial(last_kernel, columns, halves),
        name="last",
        out_shape=jax.ShapeDtypeStruct((steps, columns, features) if out_type == BF16 else (rows, features), out_type),
        in_specs=[pl.BlockSpec(memory_space=pltpu.SMEM)] + [VMEM] * (3 + len(others)),
        out_specs=VMEM,
        scratch_shapes=[pltpu.VMEM((groups // columns, rows, LANES), F32)],
        compiler_params=params(8),
        cost_estimate=pl.CostEstimate(
            flops=2 * rows * features * groups * LANES // columns, bytes_accessed=2 << 20, transcendentals=0
        ),
    )(group.reshape(1), part, w_out, lane_order(columns).T, *others)


def wide_row_scan(x, columns, halves, gain, w_u, w_bc, rate, skip):
    parts, block, width = x.shape
    items = block // columns
    inner = w_u.shape[1]
    state = rate.shape[0]
    normed = normalise(x.reshape(parts, items, columns, width), gain)
    normed = normed.transpose(0, 2, 1, 3).reshape(parts * columns, items, width)
    value = dot(normed, w_u).astype(BF16).astype(F32)
    mix = dot(normed, w_bc).astype(BF16).astype(F32)
    factor = jnp.exp(-rate)

    def advance(held, now):
        value_now, inject, readout = now
        held = factor * held + inject[:, :, None] * value_now[:, None, :]
        return held, jnp.sum(held * readout[:, :, None], axis=1) + skip * value_now

    start = jnp.zeros((items, state, inner), F32)
    _, out = lax.scan(advance, start, (value, mix[..., :state], mix[..., state:2 * state]))
    lanes = LANES // columns
    out = out.astype(BF16).reshape(parts, columns, halves, items // halves, halves, inner // (halves * lanes), lanes)
    return out.transpose(0, 4, 2, 5, 3, 1, 6).reshape(parts * halves, halves, -1, LANES)


def per_device(tokens, norm_gain, w_in, w_bc, rate_row, rate_col, skip_gain, w_out):
    height, columns, features = tokens.shape
    inner = w_out.shape[0]
    state = rate_row.shape[0]
    parts, halves = lax.axis_size("rows"), lax.axis_size("cols")
    core = lax.axis_index("cols")
    both = ("rows", "cols")
    sources = parts * halves
    items = height // sources
    group = inner // halves
    lanes = LANES // columns
    moved = lax.all_to_all(
        tokens.reshape(sources, items, columns, features), both, split_axis=0, concat_axis=0, tiled=True
    )
    scan = row_scan if items * halves % 8 == 0 and parts * columns <= 64 else wide_row_scan
    row_mixed = scan(
        moved.reshape(parts, halves * items * columns, features), columns, halves, norm_gain,
        w_in[:, :inner], w_bc[:, :2 * state], rate_row, skip_gain
    )
    back = lax.all_to_all(row_mixed, both, split_axis=0, concat_axis=0, tiled=True)

    tokens = tokens.reshape(height * columns, features)
    whole = [tokens] + [
        lax.ppermute(tokens, "cols", [(k, (k - s) % halves) for k in range(halves)]) for s in range(1, halves)
    ]
    own = core * group
    w_gate = lax.dynamic_slice_in_dim(w_in, inner + own, group, 1)
    gate, mix = home(whole, 16, columns, norm_gain, w_gate, w_bc[:, 2 * state:])
    rate = lax.dynamic_slice_in_dim(rate_col, own, group, 1)
    rate = jnp.tile(rate.reshape(state, group // lanes, lanes), (1, 1, columns))
    if items % 8 != 0:
        blocks = max(1, height // 16)
        back = back.reshape(blocks, sources // blocks, halves, group // lanes, items, LANES)
        back = back.transpose(0, 2, 3, 1, 4, 5).reshape(blocks, halves, -1, LANES)
    gated = col_scan(core.reshape(1), back, gate, mix, rate)
    out = last(core, gated[0], w_out, columns, halves, None, BF16 if halves == 1 else F32)
    for s in range(1, halves):
        arrived = lax.ppermute(gated[s], "cols", [(k, (k + s) % halves) for k in range(halves)])
        out = last((core - s) % halves, arrived, w_out, columns, halves, out, BF16 if s == halves - 1 else F32)
    return out


def solution(mesh):
    placed = (P(("slides", "cols"), "rows", None), P(), P(), P(), P(), P(), P(), P())
    return jax.shard_map(
        per_device,
        mesh=mesh,
        in_specs=placed,
        out_specs=P(("slides", "cols"), "rows", None),
        check_vma=False,
    )
```

```python
import functools

import jax
import jax.numpy as jnp
import numpy as np
from jax import lax
from jax.experimental import pallas as pl
from jax.experimental.pallas import tpu as pltpu
from jax.sharding import PartitionSpec as P

F32 = jnp.float32
BF16 = jnp.bfloat16
VMEM = pl.BlockSpec(memory_space=pltpu.VMEM)
LANES = 128
AHEAD = 3


def normalise(tokens, gain):
    as_float = tokens.astype(F32)
    scale_now = lax.rsqrt(jnp.mean(as_float * as_float, axis=-1, keepdims=True) + 1e-05)
    return (as_float * scale_now * gain).astype(BF16)


def dot(a, b):
    return jnp.dot(a, b, preferred_element_type=F32)


def params(mebibytes):
    return pltpu.CompilerParams(vmem_limit_bytes=mebibytes << 20)


def selection(shape, sources):
    matrix = np.zeros(shape, np.float32)
    matrix[np.arange(shape[0]), sources] = 1.0
    return jnp.asarray(matrix, BF16)


def row_order(items, columns):
    c, i = np.divmod(np.arange(items * columns), items)
    return selection((items * columns,) * 2, i * columns + c)


def lane_order(columns):
    part, rest = np.divmod(np.arange(columns * LANES), LANES)
    column, channel = np.divmod(rest, LANES // columns)
    return selection((columns * LANES,) * 2, column * LANES + part * (LANES // columns) + channel).T


def lane_table(columns, count):
    lane = np.arange(count * LANES)
    matrix = np.zeros((columns, count, count * LANES), np.float32)
    matrix[lane % LANES // (LANES // columns), lane // LANES, lane] = 1.0
    return jnp.asarray(matrix, BF16)


def row_kernel(parts, items, columns, halves, x_ref, gain_ref, wu_ref, wbc_ref, rate_ref, skip_ref,
               lane_ref, out_hbm, normed, b_scr, c_scr, u_all, y_all, g_scr, l_all, out_scr, p_scr, sems):
    block = items * columns
    steps = parts * columns
    rows = steps * items
    tile = u_all.shape[2]
    state = rate_ref.shape[0]
    gain = gain_ref[...]
    for part in range(parts):
        here = normalise(x_ref[part], gain).astype(F32)
        for at in range(p_scr.shape[0]):
            there = slice(at * LANES, (at + 1) * LANES)
            p_scr[at, part * block:(part + 1) * block, :] = here[:, there]
            for column in range(columns):
                first = (part * columns + column) * items
                normed[first:first + items, there] = (
                    p_scr[at, pl.ds(part * block + column, items, stride=columns), :].astype(BF16)
                )
    mix = dot(normed[...], wbc_ref[...]).astype(BF16).astype(F32)
    b_scr[...] = mix[:, :2 * state]
    c_scr[...] = mix[:, LANES:LANES + 2 * state]
    chunk = 128
    pieces = []
    at = 0
    for lag in range(steps):
        first = lag * items
        while first < rows:
            count = min(chunk, rows - first)
            pieces.append((lag, first, count, at))
            first += count
            at += count
    for lag, first, count, at in pieces:
        source = first - lag * items
        product = c_scr[first:first + count, :] * b_scr[source:source + count, :]
        g_scr[at:at + count, :] = product.astype(BF16)
    few = items // halves
    pieces_out = out_scr.shape[1]
    tiles_each = tile // LANES // pieces_out
    rows_each = out_scr.shape[4]

    def send(tile_id, piece):
        return pltpu.make_async_copy(
            out_scr.at[tile_id, piece],
            out_hbm.at[:, tile_id, :, pl.ds(piece * rows_each, rows_each), :],
            sems.at[tile_id, piece],
        )

    def one_tile(tile_id, u_scr, y_scr, l_scr):
        where = slice(tile_id * tile, (tile_id + 1) * tile)
        u_scr[...] = dot(normed[...], wu_ref[:, where]).astype(BF16).astype(F32)
        rate = rate_ref[:, where]
        skip = skip_ref[:, where]
        ones = jnp.concatenate([jnp.ones((state, LANES), BF16), jnp.zeros((state, LANES), BF16)], axis=0)
        done = 0
        table = None
        for lag, first, count, at in pieces:
            if lag != done:
                power = jnp.exp(rate * (-float(lag)))
                high = power.astype(BF16)
                low = (power - high.astype(F32)).astype(BF16)
                table = jnp.concatenate([high, low], axis=0)
                done = lag
            source = first - lag * items
            value = u_scr[source:source + count, :]
            if lag == 0:
                matrix = jnp.concatenate([dot(g_scr[at:at + count, :], ones)] * (tile // LANES), axis=1)
                y_scr[first:first + count, :] = (matrix + skip) * value
            else:
                y_scr[first:first + count, :] += dot(g_scr[at:at + count, :], table) * value
        tall = parts * items
        for part in range(parts):
            for column in range(columns):
                here = slice((part * columns + column) * items, (part * columns + column + 1) * items)
                there = slice(column * LANES, (column + 1) * LANES)
                for at in range(tile // LANES):
                    begin = at * tall + part * items
                    l_scr[begin:begin + items, there] = y_scr[here, at * LANES:(at + 1) * LANES].astype(BF16)
        for k in range(0, columns, 2):
            turned = dot(l_scr[...], lane_ref[:, k * LANES:(k + 2) * LANES])
            for at in range(tile // LANES):
                piece, first = divmod(at, tiles_each)
                begin = (first * columns + k) * few
                for part in range(parts):
                    for own in range(halves):
                        rows_at = at * tall + part * items + own * few
                        pair = jnp.concatenate(
                            [turned[rows_at:rows_at + few, j * LANES:(j + 1) * LANES] for j in range(2)], axis=0
                        )
                        out_scr[tile_id, piece, part, own, begin:begin + 2 * few, :] = pair.astype(BF16)
        for piece in range(pieces_out):
            send(tile_id, piece).start()

    for tile_id in range(halves):
        one_tile(tile_id, u_all.at[tile_id], y_all.at[tile_id], l_all.at[tile_id])
    for half in range(halves):
        for piece in range(pieces_out):
            send(half, piece).wait()


def row_scan(x, columns, halves, gain, w_u, w_bc, rate, skip):
    parts, block, width = x.shape
    items = block // columns
    inner = w_u.shape[1]
    state = rate.shape[0]
    rows = parts * block
    w_b, w_c = w_bc[:, :state], w_bc[:, state:2 * state]
    blank = jnp.zeros((width, LANES - 2 * state), BF16)
    w_mix = jnp.concatenate([w_b, w_b, blank, w_c, w_c, blank], axis=1)
    tile = inner // halves
    out_rows = tile * columns // LANES * (items // halves)
    pieces_out = 2
    out = pl.pallas_call(
        functools.partial(row_kernel, parts, items, columns, halves),
        name="row_scan",
        out_shape=jax.ShapeDtypeStruct((parts, halves, halves, out_rows, LANES), BF16),
        in_specs=[VMEM] * 7,
        out_specs=pl.BlockSpec(memory_space=pltpu.HBM),
        scratch_shapes=[
            pltpu.VMEM((rows, width), BF16),
            pltpu.VMEM((rows, 2 * state), F32),
            pltpu.VMEM((rows, 2 * state), F32),
            pltpu.VMEM((halves, rows, tile), F32),
            pltpu.VMEM((halves, rows, tile), F32),
            pltpu.VMEM((rows * (parts * columns + 1) // 2, 2 * state), BF16),
            pltpu.VMEM((halves, parts * items * tile // LANES, columns * LANES), BF16),
            pltpu.VMEM((halves, pieces_out, parts, halves, out_rows // pieces_out, LANES), BF16),
            pltpu.VMEM((width // LANES, rows, LANES), F32),
            pltpu.SemaphoreType.DMA((halves, pieces_out)),
        ],
        compiler_params=params(20),
        cost_estimate=pl.CostEstimate(
            flops=2 * rows * width * inner * 16, bytes_accessed=4 << 20, transcendentals=0
        ),
    )(x, gain[None, :], w_u, w_mix, rate, skip[None, :], lane_order(columns))
    return out.reshape(parts * halves, halves, out_rows, LANES)


def home_kernel(columns, halves, gain_ref, wz_ref, wm_ref, order_ref, lane_ref, table_ref, *refs):
    x_refs, (gate_ref, mix_ref, n_scr) = refs[:halves], refs[halves:]
    block = order_ref.shape[0]
    items = block // columns
    steps = x_refs[0].shape[0] // columns
    groups = gate_ref.shape[1] // steps
    for half, x_ref in enumerate(x_refs):
        for start in range(x_ref.shape[0] // block):
            here = normalise(x_ref[start * block:(start + 1) * block, :], gain_ref[...])
            here = dot(order_ref[...], here).astype(BF16)
            for column in range(columns):
                first = column * steps + start * items
                n_scr[first:first + items, :] = here[column * items:(column + 1) * items]
        mix = None
        project = []
        for column in range(columns):
            here = n_scr[column * steps:(column + 1) * steps, :]
            project.append(dot(here, wz_ref[...]).astype(BF16))
            part = dot(dot(here, wm_ref[...]).astype(BF16), table_ref[column])
            mix = part if mix is None else mix + part
        for n in range(mix_ref.shape[2]):
            for at in range(steps // items):
                mix_ref[half, at, n] = mix[at * items:(at + 1) * items, n * LANES:(n + 1) * LANES]
        for at in range(wz_ref.shape[1] // LANES):
            joined = jnp.concatenate([part[:, at * LANES:(at + 1) * LANES] for part in project], axis=1)
            gate = dot(joined, lane_ref[...])
            gate = gate / (1.0 + jnp.exp(-gate))
            for k in range(columns):
                gate_ref[half, pl.ds(at * columns + k, steps, stride=groups), :] = gate[:, k * LANES:(k + 1) * LANES]


def home(tokens, items, columns, gain, w_z, w_m):
    halves = len(tokens)
    rows, width = tokens[0].shape
    steps = rows // columns
    groups = w_z.shape[1] * columns // LANES
    count = w_m.shape[1]
    gate, mix = pl.pallas_call(
        functools.partial(home_kernel, columns, halves),
        name="home",
        out_shape=(
            jax.ShapeDtypeStruct((halves, steps * groups, LANES), F32),
            jax.ShapeDtypeStruct((halves, steps // items, count, items, LANES), F32),
        ),
        in_specs=[VMEM] * (6 + halves),
        out_specs=(VMEM, VMEM),
        scratch_shapes=[pltpu.VMEM((rows, width), BF16)],
        compiler_params=params(20),
        cost_estimate=pl.CostEstimate(
            flops=4 * halves * rows * width * w_z.shape[1], bytes_accessed=8 << 20, transcendentals=0
        ),
    )(gain[None, :], w_z, w_m, row_order(items, columns), lane_order(columns), lane_table(columns, count), *tokens)
    return gate.reshape(halves, steps, groups, LANES), mix


def col_kernel(state, halves, core_ref, y_hbm, gate_hbm, mix_hbm, rate_hbm, *rest):
    outs = rest[:halves]
    y_ref, gate_ref, mix_ref, out_ref, held, decay, v_scr, g_scr, sems = rest[halves:]
    per_half, _, span_steps, _ = mix_hbm.shape[1:]
    count = halves * per_half
    groups = gate_hbm.shape[2]
    take = y_hbm.shape[0] // per_half
    items = span_steps // take
    tiles = groups // 8
    spans = [slice(f * 8, f * 8 + 8) for f in range(tiles)]

    def slot_of(at):
        return lax.rem(at // per_half + halves - core_ref[0], halves)

    def copies(at):
        half, place, slot = at // per_half, at % per_half, slot_of(at)
        first = pl.multiple_of(place * span_steps, span_steps)
        return (
            pltpu.make_async_copy(y_hbm.at[pl.ds(place * take, take), half], y_ref.at[at], sems.at[at, 0]),
            pltpu.make_async_copy(mix_hbm.at[slot, place], mix_ref.at[at], sems.at[at, 1]),
            pltpu.make_async_copy(gate_hbm.at[slot, pl.ds(first, span_steps)], gate_ref.at[at], sems.at[at, 2]),
        )

    def result(at, s):
        return pltpu.make_async_copy(out_ref.at[at], outs[s].at[at % per_half], sems.at[at, 3])

    def launch(at, _):
        for copy in copies(at):
            copy.start()
        return 0

    first_copy = pltpu.make_async_copy(rate_hbm, decay, sems.at[count, 0])
    first_copy.start()
    lax.fori_loop(0, min(AHEAD, count), launch, 0)
    held[...] = jnp.zeros_like(held)
    first_copy.wait()
    decay[...] = jnp.exp(-decay[...])

    def one_span(at, _):
        for copy in copies(at):
            copy.wait()

        @pl.when(at + AHEAD < count)
        def _():
            launch(at + AHEAD, 0)

        for k in range(take):
            v_scr[k * groups * items:(k + 1) * groups * items, :] = y_ref[at, k].astype(F32)
        carry = [held[n, span, :] for n in range(state) for span in spans]
        for t in range(span_steps):
            k, i = divmod(t, items)
            value = [v_scr[pl.ds((k * groups + f * 8) * items + i, 8, stride=items), :] for f in range(tiles)]
            total = list(value)
            for n in range(state):
                b = jnp.broadcast_to(mix_ref[at, n, t:t + 1, :], (8, LANES))
                c = jnp.broadcast_to(mix_ref[at, state + n, t:t + 1, :], (8, LANES))
                for f, span in enumerate(spans):
                    h = decay[n, span, :] * carry[n * tiles + f] + b * value[f]
                    total[f] = total[f] + c * h
                    carry[n * tiles + f] = h
            for f, span in enumerate(spans):
                g_scr[pl.ds(f * 8 * span_steps + t, 8, stride=span_steps), :] = total[f] * gate_ref[at, t, span, :]
        for n in range(state):
            for f, span in enumerate(spans):
                held[n, span, :] = carry[n * tiles + f]
        out_ref[at] = g_scr[...].astype(BF16)
        for s in range(halves):
            @pl.when(slot_of(at) == s)
            def _(s=s):
                result(at, s).start()
        return 0

    lax.fori_loop(0, count, one_span, 0)

    def finish(at, _):
        for s in range(halves):
            @pl.when(slot_of(at) == s)
            def _(s=s):
                result(at, s).wait()
        return 0

    lax.fori_loop(0, count, finish, 0)


def col_scan(core, y, gate, mix, rate):
    sources, halves, rows, _ = y.shape
    state, groups, _ = rate.shape
    per_half, _, span_steps, _ = mix.shape[1:]
    count = halves * per_half
    far = pl.BlockSpec(memory_space=pltpu.HBM)
    return pl.pallas_call(
        functools.partial(col_kernel, state, halves),
        name="col_scan",
        in_specs=[pl.BlockSpec(memory_space=pltpu.SMEM)] + [far] * 4,
        out_specs=[far] * halves,
        scratch_shapes=[
            pltpu.VMEM((count, sources // per_half, rows, LANES), BF16),
            pltpu.VMEM((count, span_steps, groups, LANES), F32),
            pltpu.VMEM((count, 2 * state, span_steps, LANES), F32),
            pltpu.VMEM((count, groups * span_steps, LANES), BF16),
            pltpu.VMEM(rate.shape, F32),
            pltpu.VMEM(rate.shape, F32),
            pltpu.VMEM((span_steps * groups, LANES), F32),
            pltpu.VMEM((span_steps * groups, LANES), F32),
            pltpu.SemaphoreType.DMA((count + 1, 4)),
        ],
        out_shape=[jax.ShapeDtypeStruct((per_half, groups * span_steps, LANES), BF16)] * halves,
        compiler_params=params(62),
        cost_estimate=pl.CostEstimate(flops=5 * count * span_steps * groups * LANES * state,
                                      bytes_accessed=8 << 20, transcendentals=0),
    )(core, y, gate, mix, rate)


def last_kernel(columns, halves, group_ref, part_ref, w_ref, lane_ref, *refs):
    out_ref, l_scr = refs[-2:]
    spans, rows, _ = part_ref.shape
    width = w_ref.shape[0] // halves
    groups = width * columns // LANES
    span = rows // groups
    steps = spans * span
    for at in range(width // LANES):
        joined = jnp.concatenate([
            jnp.concatenate([
                part_ref[p, (at * columns + k) * span:(at * columns + k + 1) * span, :] for p in range(spans)
            ], axis=0) for k in range(columns)
        ], axis=1)
        turned = dot(joined, lane_ref[...])
        for column in range(columns):
            l_scr[at, pl.ds(column, steps, stride=columns), :] = turned[:, column * LANES:(column + 1) * LANES]
    first = pl.multiple_of(group_ref[0] * width, width)
    gated = jnp.concatenate([l_scr[at].astype(BF16) for at in range(width // LANES)], axis=1)
    total = dot(gated, w_ref[pl.ds(first, width), :])
    if len(refs) > 2:
        total = total + refs[0][...]
    out_ref[...] = total.reshape(out_ref.shape).astype(out_ref.dtype)


def last(group, part, w_out, columns, halves, before, out_type):
    inner, features = w_out.shape
    groups = inner * columns // (halves * LANES)
    steps = part.shape[0] * part.shape[1] // groups
    rows = steps * columns
    others = () if before is None else (before,)
    return pl.pallas_call(
        functools.partial(last_kernel, columns, halves),
        name="last",
        out_shape=jax.ShapeDtypeStruct((steps, columns, features) if out_type == BF16 else (rows, features), out_type),
        in_specs=[pl.BlockSpec(memory_space=pltpu.SMEM)] + [VMEM] * (3 + len(others)),
        out_specs=VMEM,
        scratch_shapes=[pltpu.VMEM((groups // columns, rows, LANES), F32)],
        compiler_params=params(8),
        cost_estimate=pl.CostEstimate(
            flops=2 * rows * features * groups * LANES // columns, bytes_accessed=2 << 20, transcendentals=0
        ),
    )(group.reshape(1), part, w_out, lane_order(columns).T, *others)


def wide_row_scan(x, columns, halves, gain, w_u, w_bc, rate, skip):
    parts, block, width = x.shape
    items = block // columns
    inner = w_u.shape[1]
    state = rate.shape[0]
    normed = normalise(x.reshape(parts, items, columns, width), gain)
    normed = normed.transpose(0, 2, 1, 3).reshape(parts * columns, items, width)
    value = dot(normed, w_u).astype(BF16).astype(F32)
    mix = dot(normed, w_bc).astype(BF16).astype(F32)
    factor = jnp.exp(-rate)

    def advance(held, now):
        value_now, inject, readout = now
        held = factor * held + inject[:, :, None] * value_now[:, None, :]
        return held, jnp.sum(held * readout[:, :, None], axis=1) + skip * value_now

    start = jnp.zeros((items, state, inner), F32)
    _, out = lax.scan(advance, start, (value, mix[..., :state], mix[..., state:2 * state]))
    lanes = LANES // columns
    out = out.astype(BF16).reshape(parts, columns, halves, items // halves, halves, inner // (halves * lanes), lanes)
    return out.transpose(0, 4, 2, 5, 3, 1, 6).reshape(parts * halves, halves, -1, LANES)


def per_device(tokens, norm_gain, w_in, w_bc, rate_row, rate_col, skip_gain, w_out):
    height, columns, features = tokens.shape
    inner = w_out.shape[0]
    state = rate_row.shape[0]
    parts, halves = lax.axis_size("rows"), lax.axis_size("cols")
    core = lax.axis_index("cols")
    both = ("rows", "cols")
    sources = parts * halves
    items = height // sources
    group = inner // halves
    lanes = LANES // columns
    moved = lax.all_to_all(
        tokens.reshape(sources, items, columns, features), both, split_axis=0, concat_axis=0, tiled=True
    )
    scan = row_scan if items * halves % 8 == 0 and parts * columns <= 64 else wide_row_scan
    row_mixed = scan(
        moved.reshape(parts, halves * items * columns, features), columns, halves, norm_gain,
        w_in[:, :inner], w_bc[:, :2 * state], rate_row, skip_gain
    )
    back = lax.all_to_all(row_mixed, both, split_axis=0, concat_axis=0, tiled=True)

    tokens = tokens.reshape(height * columns, features)
    whole = [tokens] + [
        lax.ppermute(tokens, "cols", [(k, (k - s) % halves) for k in range(halves)]) for s in range(1, halves)
    ]
    own = core * group
    w_gate = lax.dynamic_slice_in_dim(w_in, inner + own, group, 1)
    gate, mix = home(whole, 16, columns, norm_gain, w_gate, w_bc[:, 2 * state:])
    rate = lax.dynamic_slice_in_dim(rate_col, own, group, 1)
    rate = jnp.tile(rate.reshape(state, group // lanes, lanes), (1, 1, columns))
    if items % 8 != 0:
        blocks = max(1, height // 16)
        back = back.reshape(blocks, sources // blocks, halves, group // lanes, items, LANES)
        back = back.transpose(0, 2, 3, 1, 4, 5).reshape(blocks, halves, -1, LANES)
    gated = col_scan(core.reshape(1), back, gate, mix, rate)
    out = last(core, gated[0], w_out, columns, halves, None, BF16 if halves == 1 else F32)
    for s in range(1, halves):
        arrived = lax.ppermute(gated[s], "cols", [(k, (k + s) % halves) for k in range(halves)])
        out = last((core - s) % halves, arrived, w_out, columns, halves, out, BF16 if s == halves - 1 else F32)
    return out


def solution(mesh):
    placed = (P(("slides", "cols"), "rows", None), P(), P(), P(), P(), P(), P(), P())
    return jax.shard_map(
        per_device,
        mesh=mesh,
        in_specs=placed,
        out_specs=P(("slides", "cols"), "rows", None),
        check_vma=False,
    )
```

```python
import functools

import jax
import jax.numpy as jnp
import numpy as np
from jax import lax
from jax.experimental import pallas as pl
from jax.experimental.pallas import tpu as pltpu
from jax.sharding import PartitionSpec as P

F32 = jnp.float32
BF16 = jnp.bfloat16
VMEM = pl.BlockSpec(memory_space=pltpu.VMEM)
LANES = 128
AHEAD = 8
SPAN = 16


def normalise(tokens, gain):
    as_float = tokens.astype(F32)
    scale_now = lax.rsqrt(jnp.mean(as_float * as_float, axis=-1, keepdims=True) + 1e-05)
    return (as_float * scale_now * gain).astype(BF16)


def dot(a, b):
    return jnp.dot(a, b, preferred_element_type=F32)


def params(mebibytes):
    return pltpu.CompilerParams(vmem_limit_bytes=mebibytes << 20)


def selection(shape, sources):
    matrix = np.zeros(shape, np.float32)
    matrix[np.arange(shape[0]), sources] = 1.0
    return jnp.asarray(matrix, BF16)


def row_order(items, columns):
    c, i = np.divmod(np.arange(items * columns), items)
    return selection((items * columns,) * 2, i * columns + c)


def lane_order(columns):
    part, rest = np.divmod(np.arange(columns * LANES), LANES)
    column, channel = np.divmod(rest, LANES // columns)
    return selection((columns * LANES,) * 2, column * LANES + part * (LANES // columns) + channel).T


def lane_table(columns, count):
    lane = np.arange(count * LANES)
    matrix = np.zeros((columns, count, count * LANES), np.float32)
    matrix[lane % LANES // (LANES // columns), lane // LANES, lane] = 1.0
    return jnp.asarray(matrix, BF16)


def row_kernel(parts, items, columns, halves, x_ref, gain_ref, wu_ref, wbc_ref, rate_ref, skip_ref,
               lane_ref, out_hbm, normed, b_scr, c_scr, u_all, y_all, g_scr, l_all, out_scr, p_scr, sems):
    block = items * columns
    steps = parts * columns
    rows = steps * items
    tile = u_all.shape[2]
    state = rate_ref.shape[0]
    gain = gain_ref[...]
    for part in range(parts):
        here = normalise(x_ref[part], gain).astype(F32)
        for at in range(p_scr.shape[0]):
            there = slice(at * LANES, (at + 1) * LANES)
            p_scr[at, part * block:(part + 1) * block, :] = here[:, there]
            for column in range(columns):
                first = (part * columns + column) * items
                normed[first:first + items, there] = (
                    p_scr[at, pl.ds(part * block + column, items, stride=columns), :].astype(BF16)
                )
    mix = dot(normed[...], wbc_ref[...]).astype(BF16).astype(F32)
    b_scr[...] = mix[:, :2 * state]
    c_scr[...] = mix[:, LANES:LANES + 2 * state]
    chunk = 128
    pieces = []
    at = 0
    for lag in range(steps):
        first = lag * items
        while first < rows:
            count = min(chunk, rows - first)
            pieces.append((lag, first, count, at))
            first += count
            at += count
    for lag, first, count, at in pieces:
        source = first - lag * items
        product = c_scr[first:first + count, :] * b_scr[source:source + count, :]
        g_scr[at:at + count, :] = product.astype(BF16)
    pieces_out = out_scr.shape[1]
    tiles_each = tile // LANES // pieces_out
    rows_each = out_scr.shape[3]

    def send(tile_id, piece):
        return pltpu.make_async_copy(
            out_scr.at[tile_id, piece],
            out_hbm.at[:, tile_id, pl.ds(piece * rows_each, rows_each), :],
            sems.at[tile_id, piece],
        )

    def one_tile(tile_id, u_scr, y_scr, l_scr):
        where = slice(tile_id * tile, (tile_id + 1) * tile)
        u_scr[...] = dot(normed[...], wu_ref[:, where]).astype(BF16).astype(F32)
        rate = rate_ref[:, where]
        skip = skip_ref[:, where]
        ones = jnp.concatenate([jnp.ones((state, LANES), BF16), jnp.zeros((state, LANES), BF16)], axis=0)
        done = 0
        table = None
        for lag, first, count, at in pieces:
            if lag != done:
                power = jnp.exp(rate * (-float(lag)))
                high = power.astype(BF16)
                low = (power - high.astype(F32)).astype(BF16)
                table = jnp.concatenate([high, low], axis=0)
                done = lag
            source = first - lag * items
            value = u_scr[source:source + count, :]
            if lag == 0:
                matrix = jnp.concatenate([dot(g_scr[at:at + count, :], ones)] * (tile // LANES), axis=1)
                y_scr[first:first + count, :] = (matrix + skip) * value
            else:
                y_scr[first:first + count, :] += dot(g_scr[at:at + count, :], table) * value
        tall = parts * items
        for part in range(parts):
            for column in range(columns):
                here = slice((part * columns + column) * items, (part * columns + column + 1) * items)
                there = slice(column * LANES, (column + 1) * LANES)
                for at in range(tile // LANES):
                    begin = at * tall + part * items
                    l_scr[begin:begin + items, there] = y_scr[here, at * LANES:(at + 1) * LANES].astype(BF16)
        for k in range(0, columns, 2):
            turned = dot(l_scr[...], lane_ref[:, k * LANES:(k + 2) * LANES])
            for at in range(tile // LANES):
                piece, first = divmod(at, tiles_each)
                begin = (first * columns + k) * items
                for part in range(parts):
                    rows_at = at * tall + part * items
                    for j in range(2):
                        out_scr[tile_id, piece, part, begin + j * items:begin + (j + 1) * items, :] = (
                            turned[rows_at:rows_at + items, j * LANES:(j + 1) * LANES].astype(BF16)
                        )
        for piece in range(pieces_out):
            send(tile_id, piece).start()

    for tile_id in range(halves):
        one_tile(tile_id, u_all.at[tile_id], y_all.at[tile_id], l_all.at[tile_id])
    for half in range(halves):
        for piece in range(pieces_out):
            send(half, piece).wait()


def row_scan(x, columns, halves, gain, w_u, w_bc, rate, skip):
    parts, block, width = x.shape
    items = block // columns
    inner = w_u.shape[1]
    state = rate.shape[0]
    rows = parts * block
    w_b, w_c = w_bc[:, :state], w_bc[:, state:2 * state]
    blank = jnp.zeros((width, LANES - 2 * state), BF16)
    w_mix = jnp.concatenate([w_b, w_b, blank, w_c, w_c, blank], axis=1)
    tile = inner // halves
    out_rows = tile * columns // LANES * items
    pieces_out = 2
    out = pl.pallas_call(
        functools.partial(row_kernel, parts, items, columns, halves),
        name="row_scan",
        out_shape=jax.ShapeDtypeStruct((parts, halves, out_rows, LANES), BF16),
        in_specs=[VMEM] * 7,
        out_specs=pl.BlockSpec(memory_space=pltpu.HBM),
        scratch_shapes=[
            pltpu.VMEM((rows, width), BF16),
            pltpu.VMEM((rows, 2 * state), F32),
            pltpu.VMEM((rows, 2 * state), F32),
            pltpu.VMEM((halves, rows, tile), F32),
            pltpu.VMEM((halves, rows, tile), F32),
            pltpu.VMEM((rows * (parts * columns + 1) // 2, 2 * state), BF16),
            pltpu.VMEM((halves, parts * items * tile // LANES, columns * LANES), BF16),
            pltpu.VMEM((halves, pieces_out, parts, out_rows // pieces_out, LANES), BF16),
            pltpu.VMEM((width // LANES, rows, LANES), F32),
            pltpu.SemaphoreType.DMA((halves, pieces_out)),
        ],
        compiler_params=params(20),
        cost_estimate=pl.CostEstimate(
            flops=2 * rows * width * inner * 16, bytes_accessed=4 << 20, transcendentals=0
        ),
    )(x, gain[None, :], w_u, w_mix, rate, skip[None, :], lane_order(columns))
    return out.reshape(parts * halves, out_rows, LANES)


def home_kernel(columns, halves, gain_ref, wz_ref, wm_ref, order_ref, lane_ref, table_ref, *refs):
    x_refs, (gate_ref, mix_ref, n_scr) = refs[:halves], refs[halves:]
    block = order_ref.shape[0]
    items = block // columns
    steps = x_refs[0].shape[0] // columns
    groups = gate_ref.shape[1] // steps
    for half, x_ref in enumerate(x_refs):
        for start in range(x_ref.shape[0] // block):
            here = normalise(x_ref[start * block:(start + 1) * block, :], gain_ref[...])
            here = dot(order_ref[...], here).astype(BF16)
            for column in range(columns):
                first = column * steps + start * items
                n_scr[first:first + items, :] = here[column * items:(column + 1) * items]
        mix = None
        project = []
        for column in range(columns):
            here = n_scr[column * steps:(column + 1) * steps, :]
            project.append(dot(here, wz_ref[...]).astype(BF16))
            part = dot(dot(here, wm_ref[...]).astype(BF16), table_ref[column])
            mix = part if mix is None else mix + part
        for n in range(mix_ref.shape[2]):
            for at in range(steps // items):
                mix_ref[half, at, n] = mix[at * items:(at + 1) * items, n * LANES:(n + 1) * LANES]
        for at in range(wz_ref.shape[1] // LANES):
            joined = jnp.concatenate([part[:, at * LANES:(at + 1) * LANES] for part in project], axis=1)
            gate = dot(joined, lane_ref[...])
            gate = gate / (1.0 + jnp.exp(-gate))
            for k in range(columns):
                gate_ref[half, pl.ds(at * columns + k, steps, stride=groups), :] = gate[:, k * LANES:(k + 1) * LANES]


def home(tokens, items, columns, gain, w_z, w_m):
    halves = len(tokens)
    rows, width = tokens[0].shape
    steps = rows // columns
    groups = w_z.shape[1] * columns // LANES
    count = w_m.shape[1]
    gate, mix = pl.pallas_call(
        functools.partial(home_kernel, columns, halves),
        name="home",
        out_shape=(
            jax.ShapeDtypeStruct((halves, steps * groups, LANES), F32),
            jax.ShapeDtypeStruct((halves, steps // items, count, items, LANES), F32),
        ),
        in_specs=[VMEM] * (6 + halves),
        out_specs=(VMEM, VMEM),
        scratch_shapes=[pltpu.VMEM((rows, width), BF16)],
        compiler_params=params(20),
        cost_estimate=pl.CostEstimate(
            flops=4 * halves * rows * width * w_z.shape[1], bytes_accessed=8 << 20, transcendentals=0
        ),
    )(gain[None, :], w_z, w_m, row_order(items, columns), lane_order(columns), lane_table(columns, count), *tokens)
    return gate.reshape(halves, steps, groups, LANES), mix


def col_kernel(state, halves, core_ref, y_hbm, gate_hbm, mix_hbm, rate_hbm, *rest):
    outs = rest[:halves]
    y_ref, gate_ref, mix_ref, out_ref, held, decay, v_scr, g_scr, sems = rest[halves:]
    per_half, _, span_steps, _ = mix_hbm.shape[1:]
    count = halves * per_half
    groups = gate_hbm.shape[2]
    tiles = groups // 8
    spans = [slice(f * 8, f * 8 + 8) for f in range(tiles)]

    def slot_of(at):
        return lax.rem(at // per_half + halves - core_ref[0], halves)

    def copies(at):
        half, place, slot = at // per_half, at % per_half, slot_of(at)
        first = pl.multiple_of(place * span_steps, span_steps)
        return (
            pltpu.make_async_copy(y_hbm.at[place * halves + half], y_ref.at[at], sems.at[at, 0]),
            pltpu.make_async_copy(mix_hbm.at[slot, place], mix_ref.at[at], sems.at[at, 1]),
            pltpu.make_async_copy(gate_hbm.at[slot, pl.ds(first, span_steps)], gate_ref.at[at], sems.at[at, 2]),
        )

    def result(at, s):
        return pltpu.make_async_copy(out_ref.at[at], outs[s].at[at % per_half], sems.at[at, 3])

    def launch(at, _):
        for copy in copies(at):
            copy.start()
        return 0

    first_copy = pltpu.make_async_copy(rate_hbm, decay, sems.at[count, 0])
    first_copy.start()
    lax.fori_loop(0, min(AHEAD, count), launch, 0)
    held[...] = jnp.zeros_like(held)
    first_copy.wait()
    decay[...] = jnp.exp(-decay[...])

    def one_span(at, _):
        for copy in copies(at):
            copy.wait()

        @pl.when(at + AHEAD < count)
        def _():
            launch(at + AHEAD, 0)

        v_scr[...] = y_ref[at].astype(F32)
        carry = [held[n, span, :] for n in range(state) for span in spans]
        for t in range(span_steps):
            value = [v_scr[pl.ds(f * 8 * span_steps + t, 8, stride=span_steps), :] for f in range(tiles)]
            total = list(value)
            for n in range(state):
                b = jnp.broadcast_to(mix_ref[at, n, t:t + 1, :], (8, LANES))
                c = jnp.broadcast_to(mix_ref[at, state + n, t:t + 1, :], (8, LANES))
                for f, span in enumerate(spans):
                    h = decay[n, span, :] * carry[n * tiles + f] + b * value[f]
                    total[f] = total[f] + c * h
                    carry[n * tiles + f] = h
            for f, span in enumerate(spans):
                g_scr[pl.ds(f * 8 * span_steps + t, 8, stride=span_steps), :] = total[f] * gate_ref[at, t, span, :]
        for n in range(state):
            for f, span in enumerate(spans):
                held[n, span, :] = carry[n * tiles + f]
        out_ref[at] = g_scr[...].astype(BF16)
        for s in range(halves):
            @pl.when(slot_of(at) == s)
            def _(s=s):
                result(at, s).start()
        return 0

    lax.fori_loop(0, count, one_span, 0)

    def finish(at, _):
        for s in range(halves):
            @pl.when(slot_of(at) == s)
            def _(s=s):
                result(at, s).wait()
        return 0

    lax.fori_loop(0, count, finish, 0)


def col_scan(core, y, gate, mix, rate):
    state, groups, _ = rate.shape
    halves, per_half, _, span_steps, _ = mix.shape
    count = halves * per_half
    far = pl.BlockSpec(memory_space=pltpu.HBM)
    return pl.pallas_call(
        functools.partial(col_kernel, state, halves),
        name="col_scan",
        in_specs=[pl.BlockSpec(memory_space=pltpu.SMEM)] + [far] * 4,
        out_specs=[far] * halves,
        scratch_shapes=[
            pltpu.VMEM((count, groups * span_steps, LANES), BF16),
            pltpu.VMEM((count, span_steps, groups, LANES), F32),
            pltpu.VMEM((count, 2 * state, span_steps, LANES), F32),
            pltpu.VMEM((count, groups * span_steps, LANES), BF16),
            pltpu.VMEM(rate.shape, F32),
            pltpu.VMEM(rate.shape, F32),
            pltpu.VMEM((span_steps * groups, LANES), F32),
            pltpu.VMEM((span_steps * groups, LANES), F32),
            pltpu.SemaphoreType.DMA((count + 1, 4)),
        ],
        out_shape=[jax.ShapeDtypeStruct((per_half, groups * span_steps, LANES), BF16)] * halves,
        compiler_params=params(62),
        cost_estimate=pl.CostEstimate(flops=5 * count * span_steps * groups * LANES * state,
                                      bytes_accessed=8 << 20, transcendentals=0),
    )(core, y, gate, mix, rate)


def last_kernel(columns, halves, group_ref, part_ref, w_ref, lane_ref, *refs):
    out_ref, l_scr = refs[-2:]
    spans, rows, _ = part_ref.shape
    width = w_ref.shape[0] // halves
    groups = width * columns // LANES
    span = rows // groups
    steps = spans * span
    for at in range(width // LANES):
        joined = jnp.concatenate([
            jnp.concatenate([
                part_ref[p, (at * columns + k) * span:(at * columns + k + 1) * span, :] for p in range(spans)
            ], axis=0) for k in range(columns)
        ], axis=1)
        turned = dot(joined, lane_ref[...])
        for column in range(columns):
            l_scr[at, pl.ds(column, steps, stride=columns), :] = turned[:, column * LANES:(column + 1) * LANES]
    first = pl.multiple_of(group_ref[0] * width, width)
    gated = jnp.concatenate([l_scr[at].astype(BF16) for at in range(width // LANES)], axis=1)
    total = dot(gated, w_ref[pl.ds(first, width), :])
    if len(refs) > 2:
        total = total + refs[0][...]
    out_ref[...] = total.reshape(out_ref.shape).astype(out_ref.dtype)


def last(group, part, w_out, columns, halves, before, out_type):
    inner, features = w_out.shape
    groups = inner * columns // (halves * LANES)
    steps = part.shape[0] * part.shape[1] // groups
    rows = steps * columns
    others = () if before is None else (before,)
    return pl.pallas_call(
        functools.partial(last_kernel, columns, halves),
        name="last",
        out_shape=jax.ShapeDtypeStruct((steps, columns, features) if out_type == BF16 else (rows, features), out_type),
        in_specs=[pl.BlockSpec(memory_space=pltpu.SMEM)] + [VMEM] * (3 + len(others)),
        out_specs=VMEM,
        scratch_shapes=[pltpu.VMEM((groups // columns, rows, LANES), F32)],
        compiler_params=params(8),
        cost_estimate=pl.CostEstimate(
            flops=2 * rows * features * groups * LANES // columns, bytes_accessed=2 << 20, transcendentals=0
        ),
    )(group.reshape(1), part, w_out, lane_order(columns).T, *others)


def wide_row_scan(x, columns, halves, gain, w_u, w_bc, rate, skip):
    parts, block, width = x.shape
    items = block // columns
    inner = w_u.shape[1]
    state = rate.shape[0]
    normed = normalise(x.reshape(parts, items, columns, width), gain)
    normed = normed.transpose(0, 2, 1, 3).reshape(parts * columns, items, width)
    value = dot(normed, w_u).astype(BF16).astype(F32)
    mix = dot(normed, w_bc).astype(BF16).astype(F32)
    factor = jnp.exp(-rate)

    def advance(held, now):
        value_now, inject, readout = now
        held = factor * held + inject[:, :, None] * value_now[:, None, :]
        return held, jnp.sum(held * readout[:, :, None], axis=1) + skip * value_now

    start = jnp.zeros((items, state, inner), F32)
    _, out = lax.scan(advance, start, (value, mix[..., :state], mix[..., state:2 * state]))
    lanes = LANES // columns
    out = out.astype(BF16).reshape(parts, columns, items, halves, inner // (halves * lanes), lanes)
    return out.transpose(0, 3, 4, 2, 1, 5).reshape(parts * halves, -1, LANES)


def per_device(tokens, norm_gain, w_in, w_bc, rate_row, rate_col, skip_gain, w_out):
    height, columns, features = tokens.shape
    inner = w_out.shape[0]
    state = rate_row.shape[0]
    parts, halves = lax.axis_size("rows"), lax.axis_size("cols")
    core = lax.axis_index("cols")
    both = ("rows", "cols")
    items = height // parts
    group = inner // halves
    lanes = LANES // columns
    moved = lax.all_to_all(
        tokens.reshape(parts, items, columns, features), "rows", split_axis=0, concat_axis=0, tiled=True
    )
    scan = row_scan if items == SPAN and parts * columns <= 64 else wide_row_scan
    row_mixed = scan(
        moved.reshape(parts, items * columns, features), columns, halves, norm_gain,
        w_in[:, :inner], w_bc[:, :2 * state], rate_row, skip_gain
    )
    back = lax.all_to_all(row_mixed, both, split_axis=0, concat_axis=0, tiled=True)

    tokens = tokens.reshape(height * columns, features)
    whole = [tokens] + [
        lax.ppermute(tokens, "cols", [(k, (k - s) % halves) for k in range(halves)]) for s in range(1, halves)
    ]
    own = core * group
    w_gate = lax.dynamic_slice_in_dim(w_in, inner + own, group, 1)
    gate, mix = home(whole, SPAN, columns, norm_gain, w_gate, w_bc[:, 2 * state:])
    rate = lax.dynamic_slice_in_dim(rate_col, own, group, 1)
    rate = jnp.tile(rate.reshape(state, group // lanes, lanes), (1, 1, columns))
    if items != SPAN:
        spans = height // SPAN
        back = back.reshape(spans, parts // spans, halves, group // lanes, items, LANES)
        back = back.transpose(0, 2, 3, 1, 4, 5).reshape(spans * halves, -1, LANES)
    gated = col_scan(core.reshape(1), back, gate, mix, rate)
    out = last(core, gated[0], w_out, columns, halves, None, BF16 if halves == 1 else F32)
    for s in range(1, halves):
        arrived = lax.ppermute(gated[s], "cols", [(k, (k + s) % halves) for k in range(halves)])
        out = last((core - s) % halves, arrived, w_out, columns, halves, out, BF16 if s == halves - 1 else F32)
    return out


def solution(mesh):
    placed = (P(("slides", "cols"), "rows", None), P(), P(), P(), P(), P(), P(), P())
    return jax.shard_map(
        per_device,
        mesh=mesh,
        in_specs=placed,
        out_specs=P(("slides", "cols"), "rows", None),
        check_vma=False,
    )
```

```python
import functools

import jax
import jax.numpy as jnp
import numpy as np
from jax import lax
from jax.experimental import pallas as pl
from jax.experimental.pallas import tpu as pltpu
from jax.sharding import PartitionSpec as P

F32 = jnp.float32
BF16 = jnp.bfloat16
VMEM = pl.BlockSpec(memory_space=pltpu.VMEM)
LANES = 128
SPAN = 16


def normalise(tokens, gain):
    as_float = tokens.astype(F32)
    scale_now = lax.rsqrt(jnp.mean(as_float * as_float, axis=-1, keepdims=True) + 1e-05)
    return (as_float * scale_now * gain).astype(BF16)


def dot(a, b):
    return jnp.dot(a, b, preferred_element_type=F32)


def params(mebibytes):
    return pltpu.CompilerParams(vmem_limit_bytes=mebibytes << 20)


def selection(shape, sources):
    matrix = np.zeros(shape, np.float32)
    matrix[np.arange(shape[0]), sources] = 1.0
    return jnp.asarray(matrix, BF16)


def row_order(items, columns):
    c, i = np.divmod(np.arange(items * columns), items)
    return selection((items * columns,) * 2, i * columns + c)


def lane_order(columns):
    part, rest = np.divmod(np.arange(columns * LANES), LANES)
    column, channel = np.divmod(rest, LANES // columns)
    return selection((columns * LANES,) * 2, column * LANES + part * (LANES // columns) + channel).T


def lane_table(columns, count):
    lane = np.arange(count * LANES)
    matrix = np.zeros((columns, count, count * LANES), np.float32)
    matrix[lane % LANES // (LANES // columns), lane // LANES, lane] = 1.0
    return jnp.asarray(matrix, BF16)


def row_kernel(parts, items, columns, halves, x_ref, gain_ref, wu_ref, wbc_ref, rate_ref, skip_ref,
               lane_ref, out_hbm, normed, b_scr, c_scr, u_all, y_all, g_scr, l_all, out_scr, p_scr, sems):
    block = items * columns
    steps = parts * columns
    rows = steps * items
    tile = u_all.shape[2]
    state = rate_ref.shape[0]
    gain = gain_ref[...]
    for part in range(parts):
        here = normalise(x_ref[part], gain).astype(F32)
        for at in range(p_scr.shape[0]):
            there = slice(at * LANES, (at + 1) * LANES)
            p_scr[at, part * block:(part + 1) * block, :] = here[:, there]
            for column in range(columns):
                first = (part * columns + column) * items
                normed[first:first + items, there] = (
                    p_scr[at, pl.ds(part * block + column, items, stride=columns), :].astype(BF16)
                )
    mix = dot(normed[...], wbc_ref[...]).astype(BF16).astype(F32)
    b_scr[...] = mix[:, :2 * state]
    c_scr[...] = mix[:, LANES:LANES + 2 * state]
    chunk = 128
    pieces = []
    at = 0
    for lag in range(steps):
        first = lag * items
        while first < rows:
            count = min(chunk, rows - first)
            pieces.append((lag, first, count, at))
            first += count
            at += count
    for lag, first, count, at in pieces:
        source = first - lag * items
        product = c_scr[first:first + count, :] * b_scr[source:source + count, :]
        g_scr[at:at + count, :] = product.astype(BF16)
    pieces_out = out_scr.shape[1]
    tiles_each = tile // LANES // pieces_out
    rows_each = out_scr.shape[3]

    def send(tile_id, piece):
        return pltpu.make_async_copy(
            out_scr.at[tile_id, piece],
            out_hbm.at[:, tile_id, pl.ds(piece * rows_each, rows_each), :],
            sems.at[tile_id, piece],
        )

    def one_tile(tile_id, u_scr, y_scr, l_scr):
        where = slice(tile_id * tile, (tile_id + 1) * tile)
        u_scr[...] = dot(normed[...], wu_ref[:, where]).astype(BF16).astype(F32)
        rate = rate_ref[:, where]
        skip = skip_ref[:, where]
        ones = jnp.concatenate([jnp.ones((state, LANES), BF16), jnp.zeros((state, LANES), BF16)], axis=0)
        done = 0
        table = None
        for lag, first, count, at in pieces:
            if lag != done:
                power = jnp.exp(rate * (-float(lag)))
                high = power.astype(BF16)
                low = (power - high.astype(F32)).astype(BF16)
                table = jnp.concatenate([high, low], axis=0)
                done = lag
            source = first - lag * items
            value = u_scr[source:source + count, :]
            if lag == 0:
                matrix = jnp.concatenate([dot(g_scr[at:at + count, :], ones)] * (tile // LANES), axis=1)
                y_scr[first:first + count, :] = (matrix + skip) * value
            else:
                y_scr[first:first + count, :] += dot(g_scr[at:at + count, :], table) * value
        tall = parts * items
        for part in range(parts):
            for column in range(columns):
                here = slice((part * columns + column) * items, (part * columns + column + 1) * items)
                there = slice(column * LANES, (column + 1) * LANES)
                for at in range(tile // LANES):
                    begin = at * tall + part * items
                    l_scr[begin:begin + items, there] = y_scr[here, at * LANES:(at + 1) * LANES].astype(BF16)
        for k in range(0, columns, 2):
            turned = dot(l_scr[...], lane_ref[:, k * LANES:(k + 2) * LANES])
            for at in range(tile // LANES):
                piece, first = divmod(at, tiles_each)
                begin = (first * columns + k) * items
                for part in range(parts):
                    rows_at = at * tall + part * items
                    for j in range(2):
                        out_scr[tile_id, piece, part, begin + j * items:begin + (j + 1) * items, :] = (
                            turned[rows_at:rows_at + items, j * LANES:(j + 1) * LANES].astype(BF16)
                        )
        for piece in range(pieces_out):
            send(tile_id, piece).start()

    for tile_id in range(halves):
        one_tile(tile_id, u_all.at[tile_id], y_all.at[tile_id], l_all.at[tile_id])
    for half in range(halves):
        for piece in range(pieces_out):
            send(half, piece).wait()


def row_scan(x, columns, halves, gain, w_u, w_bc, rate, skip):
    parts, block, width = x.shape
    items = block // columns
    inner = w_u.shape[1]
    state = rate.shape[0]
    rows = parts * block
    w_b, w_c = w_bc[:, :state], w_bc[:, state:2 * state]
    blank = jnp.zeros((width, LANES - 2 * state), BF16)
    w_mix = jnp.concatenate([w_b, w_b, blank, w_c, w_c, blank], axis=1)
    tile = inner // halves
    out_rows = tile * columns // LANES * items
    pieces_out = 2
    out = pl.pallas_call(
        functools.partial(row_kernel, parts, items, columns, halves),
        name="row_scan",
        out_shape=jax.ShapeDtypeStruct((parts, halves, out_rows, LANES), BF16),
        in_specs=[VMEM] * 7,
        out_specs=pl.BlockSpec(memory_space=pltpu.HBM),
        scratch_shapes=[
            pltpu.VMEM((rows, width), BF16),
            pltpu.VMEM((rows, 2 * state), F32),
            pltpu.VMEM((rows, 2 * state), F32),
            pltpu.VMEM((halves, rows, tile), F32),
            pltpu.VMEM((halves, rows, tile), F32),
            pltpu.VMEM((rows * (parts * columns + 1) // 2, 2 * state), BF16),
            pltpu.VMEM((halves, parts * items * tile // LANES, columns * LANES), BF16),
            pltpu.VMEM((halves, pieces_out, parts, out_rows // pieces_out, LANES), BF16),
            pltpu.VMEM((width // LANES, rows, LANES), F32),
            pltpu.SemaphoreType.DMA((halves, pieces_out)),
        ],
        compiler_params=params(20),
        cost_estimate=pl.CostEstimate(
            flops=2 * rows * width * inner * 16, bytes_accessed=4 << 20, transcendentals=0
        ),
    )(x, gain[None, :], w_u, w_mix, rate, skip[None, :], lane_order(columns))
    return out.reshape(parts * halves, out_rows, LANES)


def home_kernel(columns, halves, gain_ref, wz_ref, wm_ref, order_ref, lane_ref, table_ref, *refs):
    x_refs, (gate_ref, mix_ref, n_scr) = refs[:halves], refs[halves:]
    block = order_ref.shape[0]
    items = block // columns
    steps = x_refs[0].shape[0] // columns
    groups = gate_ref.shape[1] // steps
    for half, x_ref in enumerate(x_refs):
        for start in range(x_ref.shape[0] // block):
            here = normalise(x_ref[start * block:(start + 1) * block, :], gain_ref[...])
            here = dot(order_ref[...], here).astype(BF16)
            for column in range(columns):
                first = column * steps + start * items
                n_scr[first:first + items, :] = here[column * items:(column + 1) * items]
        mix = None
        project = []
        for column in range(columns):
            here = n_scr[column * steps:(column + 1) * steps, :]
            project.append(dot(here, wz_ref[...]).astype(BF16))
            part = dot(dot(here, wm_ref[...]).astype(BF16), table_ref[column])
            mix = part if mix is None else mix + part
        for n in range(mix_ref.shape[2]):
            for at in range(steps // items):
                mix_ref[half, at, n] = mix[at * items:(at + 1) * items, n * LANES:(n + 1) * LANES]
        for at in range(wz_ref.shape[1] // LANES):
            joined = jnp.concatenate([part[:, at * LANES:(at + 1) * LANES] for part in project], axis=1)
            gate = dot(joined, lane_ref[...])
            gate = gate / (1.0 + jnp.exp(-gate))
            for k in range(columns):
                gate_ref[half, pl.ds(at * columns + k, steps, stride=groups), :] = gate[:, k * LANES:(k + 1) * LANES]


def home(tokens, items, columns, gain, w_z, w_m):
    halves = len(tokens)
    rows, width = tokens[0].shape
    steps = rows // columns
    groups = w_z.shape[1] * columns // LANES
    count = w_m.shape[1]
    gate, mix = pl.pallas_call(
        functools.partial(home_kernel, columns, halves),
        name="home",
        out_shape=(
            jax.ShapeDtypeStruct((halves, steps * groups, LANES), F32),
            jax.ShapeDtypeStruct((halves, steps // items, count, items, LANES), F32),
        ),
        in_specs=[VMEM] * (6 + halves),
        out_specs=(VMEM, VMEM),
        scratch_shapes=[pltpu.VMEM((rows, width), BF16)],
        compiler_params=params(20),
        cost_estimate=pl.CostEstimate(
            flops=4 * halves * rows * width * w_z.shape[1], bytes_accessed=8 << 20, transcendentals=0
        ),
    )(gain[None, :], w_z, w_m, row_order(items, columns), lane_order(columns), lane_table(columns, count), *tokens)
    return gate.reshape(halves, steps, groups, LANES), mix


def col_kernel(state, halves, core_ref, y_hbm, gate_hbm, mix_hbm, rate_hbm, *rest):
    outs = rest[:halves]
    y_ref, gate_ref, mix_ref, out_ref, held, decay, v_scr, g_scr, sems = rest[halves:]
    per_half, _, span_steps, _ = mix_hbm.shape[1:]
    count = halves * per_half
    groups = gate_hbm.shape[2]
    tiles = groups // 8
    spans = [slice(f * 8, f * 8 + 8) for f in range(tiles)]

    def slot_of(half):
        return lax.rem(half + halves - core_ref[0], halves)

    def copies(half, slot, place):
        at = half * per_half + place
        first = pl.multiple_of(place * span_steps, span_steps)
        return (
            pltpu.make_async_copy(y_hbm.at[place * halves + half], y_ref.at[at], sems.at[at, 0]),
            pltpu.make_async_copy(mix_hbm.at[slot, place], mix_ref.at[at], sems.at[at, 1]),
            pltpu.make_async_copy(gate_hbm.at[slot, pl.ds(first, span_steps)], gate_ref.at[at], sems.at[at, 2]),
        )

    def result(half, place, s):
        at = half * per_half + place
        return pltpu.make_async_copy(out_ref.at[at], outs[s].at[place], sems.at[at, 3])

    def launch(half, slot, place):
        for copy in copies(half, slot, place):
            copy.start()

    first_copy = pltpu.make_async_copy(rate_hbm, decay, sems.at[count, 0])
    first_copy.start()
    first_slot = slot_of(0)

    def launch_first(place, _):
        launch(0, first_slot, place)
        return 0

    lax.fori_loop(0, per_half, launch_first, 0)
    held[...] = jnp.zeros_like(held)
    first_copy.wait()
    decay[...] = jnp.exp(-decay[...])

    def one_span(half, slot, next_slot, place):
        at = half * per_half + place
        for copy in copies(half, slot, place):
            copy.wait()

        @pl.when(half + 1 < halves)
        def _():
            launch(half + 1, next_slot, place)

        v_scr[...] = y_ref[at].astype(F32)
        carry = [held[n, span, :] for n in range(state) for span in spans]
        for t in range(span_steps):
            value = [v_scr[pl.ds(f * 8 * span_steps + t, 8, stride=span_steps), :] for f in range(tiles)]
            total = list(value)
            for n in range(state):
                b = jnp.broadcast_to(mix_ref[at, n, t:t + 1, :], (8, LANES))
                c = jnp.broadcast_to(mix_ref[at, state + n, t:t + 1, :], (8, LANES))
                for f, span in enumerate(spans):
                    h = decay[n, span, :] * carry[n * tiles + f] + b * value[f]
                    total[f] = total[f] + c * h
                    carry[n * tiles + f] = h
            for f, span in enumerate(spans):
                g_scr[pl.ds(f * 8 * span_steps + t, 8, stride=span_steps), :] = total[f] * gate_ref[at, t, span, :]
        for n in range(state):
            for f, span in enumerate(spans):
                held[n, span, :] = carry[n * tiles + f]
        out_ref[at] = g_scr[...].astype(BF16)
        for s in range(halves):
            @pl.when(slot == s)
            def _(s=s):
                result(half, place, s).start()

    def one_half(half, _):
        slot, next_slot = slot_of(half), slot_of(half + 1)

        def step(place, _):
            one_span(half, slot, next_slot, place)
            return 0

        return lax.fori_loop(0, per_half, step, 0)

    lax.fori_loop(0, halves, one_half, 0)

    def finish(half, _):
        for s in range(halves):
            @pl.when(slot_of(half) == s)
            def _(s=s):
                for place in range(per_half):
                    result(half, place, s).wait()
        return 0

    lax.fori_loop(0, halves, finish, 0)


def col_scan(core, y, gate, mix, rate):
    state, groups, _ = rate.shape
    halves, per_half, _, span_steps, _ = mix.shape
    count = halves * per_half
    far = pl.BlockSpec(memory_space=pltpu.HBM)
    return pl.pallas_call(
        functools.partial(col_kernel, state, halves),
        name="col_scan",
        in_specs=[pl.BlockSpec(memory_space=pltpu.SMEM)] + [far] * 4,
        out_specs=[far] * halves,
        scratch_shapes=[
            pltpu.VMEM((count, groups * span_steps, LANES), BF16),
            pltpu.VMEM((count, span_steps, groups, LANES), F32),
            pltpu.VMEM((count, 2 * state, span_steps, LANES), F32),
            pltpu.VMEM((count, groups * span_steps, LANES), BF16),
            pltpu.VMEM(rate.shape, F32),
            pltpu.VMEM(rate.shape, F32),
            pltpu.VMEM((span_steps * groups, LANES), F32),
            pltpu.VMEM((span_steps * groups, LANES), F32),
            pltpu.SemaphoreType.DMA((count + 1, 4)),
        ],
        out_shape=[jax.ShapeDtypeStruct((per_half, groups * span_steps, LANES), BF16)] * halves,
        compiler_params=params(62),
        cost_estimate=pl.CostEstimate(flops=5 * count * span_steps * groups * LANES * state,
                                      bytes_accessed=8 << 20, transcendentals=0),
    )(core, y, gate, mix, rate)


def last_kernel(columns, halves, group_ref, part_ref, w_ref, lane_ref, *refs):
    out_ref, l_scr = refs[-2:]
    spans, rows, _ = part_ref.shape
    width = w_ref.shape[0] // halves
    groups = width * columns // LANES
    span = rows // groups
    steps = spans * span
    for at in range(width // LANES):
        joined = jnp.concatenate([
            jnp.concatenate([
                part_ref[p, (at * columns + k) * span:(at * columns + k + 1) * span, :] for p in range(spans)
            ], axis=0) for k in range(columns)
        ], axis=1)
        turned = dot(joined, lane_ref[...])
        for column in range(columns):
            l_scr[at, pl.ds(column, steps, stride=columns), :] = turned[:, column * LANES:(column + 1) * LANES]
    first = pl.multiple_of(group_ref[0] * width, width)
    gated = jnp.concatenate([l_scr[at].astype(BF16) for at in range(width // LANES)], axis=1)
    total = dot(gated, w_ref[pl.ds(first, width), :])
    if len(refs) > 2:
        total = total + refs[0][...]
    out_ref[...] = total.reshape(out_ref.shape).astype(out_ref.dtype)


def last(group, part, w_out, columns, halves, before, out_type):
    inner, features = w_out.shape
    groups = inner * columns // (halves * LANES)
    steps = part.shape[0] * part.shape[1] // groups
    rows = steps * columns
    others = () if before is None else (before,)
    return pl.pallas_call(
        functools.partial(last_kernel, columns, halves),
        name="last",
        out_shape=jax.ShapeDtypeStruct((steps, columns, features) if out_type == BF16 else (rows, features), out_type),
        in_specs=[pl.BlockSpec(memory_space=pltpu.SMEM)] + [VMEM] * (3 + len(others)),
        out_specs=VMEM,
        scratch_shapes=[pltpu.VMEM((groups // columns, rows, LANES), F32)],
        compiler_params=params(8),
        cost_estimate=pl.CostEstimate(
            flops=2 * rows * features * groups * LANES // columns, bytes_accessed=2 << 20, transcendentals=0
        ),
    )(group.reshape(1), part, w_out, lane_order(columns).T, *others)


def wide_row_scan(x, columns, halves, gain, w_u, w_bc, rate, skip):
    parts, block, width = x.shape
    items = block // columns
    inner = w_u.shape[1]
    state = rate.shape[0]
    normed = normalise(x.reshape(parts, items, columns, width), gain)
    normed = normed.transpose(0, 2, 1, 3).reshape(parts * columns, items, width)
    value = dot(normed, w_u).astype(BF16).astype(F32)
    mix = dot(normed, w_bc).astype(BF16).astype(F32)
    factor = jnp.exp(-rate)

    def advance(held, now):
        value_now, inject, readout = now
        held = factor * held + inject[:, :, None] * value_now[:, None, :]
        return held, jnp.sum(held * readout[:, :, None], axis=1) + skip * value_now

    start = jnp.zeros((items, state, inner), F32)
    _, out = lax.scan(advance, start, (value, mix[..., :state], mix[..., state:2 * state]))
    lanes = LANES // columns
    out = out.astype(BF16).reshape(parts, columns, items, halves, inner // (halves * lanes), lanes)
    return out.transpose(0, 3, 4, 2, 1, 5).reshape(parts * halves, -1, LANES)


def per_device(tokens, norm_gain, w_in, w_bc, rate_row, rate_col, skip_gain, w_out):
    height, columns, features = tokens.shape
    inner = w_out.shape[0]
    state = rate_row.shape[0]
    parts, halves = lax.axis_size("rows"), lax.axis_size("cols")
    core = lax.axis_index("cols")
    both = ("rows", "cols")
    items = height // parts
    group = inner // halves
    lanes = LANES // columns
    moved = lax.all_to_all(
        tokens.reshape(parts, items, columns, features), "rows", split_axis=0, concat_axis=0, tiled=True
    )
    scan = row_scan if items == SPAN and parts * columns <= 64 else wide_row_scan
    row_mixed = scan(
        moved.reshape(parts, items * columns, features), columns, halves, norm_gain,
        w_in[:, :inner], w_bc[:, :2 * state], rate_row, skip_gain
    )
    back = lax.all_to_all(row_mixed, both, split_axis=0, concat_axis=0, tiled=True)

    tokens = tokens.reshape(height * columns, features)
    whole = [tokens] + [
        lax.ppermute(tokens, "cols", [(k, (k - s) % halves) for k in range(halves)]) for s in range(1, halves)
    ]
    own = core * group
    w_gate = lax.dynamic_slice_in_dim(w_in, inner + own, group, 1)
    gate, mix = home(whole, SPAN, columns, norm_gain, w_gate, w_bc[:, 2 * state:])
    rate = lax.dynamic_slice_in_dim(rate_col, own, group, 1)
    rate = jnp.tile(rate.reshape(state, group // lanes, lanes), (1, 1, columns))
    if items != SPAN:
        spans = height // SPAN
        back = back.reshape(spans, parts // spans, halves, group // lanes, items, LANES)
        back = back.transpose(0, 2, 3, 1, 4, 5).reshape(spans * halves, -1, LANES)
    gated = col_scan(core.reshape(1), back, gate, mix, rate)
    out = last(core, gated[0], w_out, columns, halves, None, BF16 if halves == 1 else F32)
    for s in range(1, halves):
        arrived = lax.ppermute(gated[s], "cols", [(k, (k + s) % halves) for k in range(halves)])
        out = last((core - s) % halves, arrived, w_out, columns, halves, out, BF16 if s == halves - 1 else F32)
    return out


def solution(mesh):
    placed = (P(("slides", "cols"), "rows", None), P(), P(), P(), P(), P(), P(), P())
    return jax.shard_map(
        per_device,
        mesh=mesh,
        in_specs=placed,
        out_specs=P(("slides", "cols"), "rows", None),
        check_vma=False,
    )
```

```python
import functools

import jax
import jax.numpy as jnp
import numpy as np
from jax import lax
from jax.experimental import pallas as pl
from jax.experimental.pallas import tpu as pltpu
from jax.sharding import PartitionSpec as P

F32 = jnp.float32
BF16 = jnp.bfloat16
VMEM = pl.BlockSpec(memory_space=pltpu.VMEM)
LANES = 128
AHEAD = 8
SPAN = 16


def normalise(tokens, gain):
    as_float = tokens.astype(F32)
    scale_now = lax.rsqrt(jnp.mean(as_float * as_float, axis=-1, keepdims=True) + 1e-05)
    return (as_float * scale_now * gain).astype(BF16)


def dot(a, b):
    return jnp.dot(a, b, preferred_element_type=F32)


def params(mebibytes):
    return pltpu.CompilerParams(vmem_limit_bytes=mebibytes << 20)


def selection(shape, sources):
    matrix = np.zeros(shape, np.float32)
    matrix[np.arange(shape[0]), sources] = 1.0
    return jnp.asarray(matrix, BF16)


def row_order(items, columns):
    c, i = np.divmod(np.arange(items * columns), items)
    return selection((items * columns,) * 2, i * columns + c)


def lane_order(columns):
    part, rest = np.divmod(np.arange(columns * LANES), LANES)
    column, channel = np.divmod(rest, LANES // columns)
    return selection((columns * LANES,) * 2, column * LANES + part * (LANES // columns) + channel).T


def lane_table(columns, count):
    lane = np.arange(count * LANES)
    matrix = np.zeros((columns, count, count * LANES), np.float32)
    matrix[lane % LANES // (LANES // columns), lane // LANES, lane] = 1.0
    return jnp.asarray(matrix, BF16)


def row_kernel(parts, items, columns, halves, x_ref, gain_ref, wu_ref, wbc_ref, rate_ref, skip_ref,
               lane_ref, out_hbm, normed, b_scr, c_scr, u_all, y_all, g_scr, l_all, out_scr, p_scr, sems):
    block = items * columns
    steps = parts * columns
    rows = steps * items
    tile = u_all.shape[2]
    state = rate_ref.shape[0]
    gain = gain_ref[...]
    for part in range(parts):
        here = normalise(x_ref[part], gain).astype(F32)
        for at in range(p_scr.shape[0]):
            there = slice(at * LANES, (at + 1) * LANES)
            p_scr[at, part * block:(part + 1) * block, :] = here[:, there]
            for column in range(columns):
                first = (part * columns + column) * items
                normed[first:first + items, there] = (
                    p_scr[at, pl.ds(part * block + column, items, stride=columns), :].astype(BF16)
                )
    mix = dot(normed[...], wbc_ref[...]).astype(BF16).astype(F32)
    b_scr[...] = mix[:, :2 * state]
    c_scr[...] = mix[:, LANES:LANES + 2 * state]
    chunk = 256
    pieces = []
    at = 0
    for lag in range(steps):
        first = lag * items
        while first < rows:
            count = min(chunk, rows - first)
            pieces.append((lag, first, count, at))
            first += count
            at += count
    for lag, first, count, at in pieces:
        source = first - lag * items
        product = c_scr[first:first + count, :] * b_scr[source:source + count, :]
        g_scr[at:at + count, :] = product.astype(BF16)
    pieces_out = out_scr.shape[1]
    tiles_each = tile // LANES // pieces_out
    rows_each = out_scr.shape[3]

    def send(tile_id, piece):
        return pltpu.make_async_copy(
            out_scr.at[tile_id, piece],
            out_hbm.at[:, tile_id, pl.ds(piece * rows_each, rows_each), :],
            sems.at[tile_id, piece],
        )

    def one_tile(tile_id, u_scr, y_scr, l_scr):
        where = slice(tile_id * tile, (tile_id + 1) * tile)
        u_scr[...] = dot(normed[...], wu_ref[:, where]).astype(BF16).astype(F32)
        rate = rate_ref[:, where]
        skip = skip_ref[:, where]
        ones = jnp.concatenate([jnp.ones((state, LANES), BF16), jnp.zeros((state, LANES), BF16)], axis=0)
        done = 0
        table = None
        for lag, first, count, at in pieces:
            if lag != done:
                power = jnp.exp(rate * (-float(lag)))
                high = power.astype(BF16)
                low = (power - high.astype(F32)).astype(BF16)
                table = jnp.concatenate([high, low], axis=0)
                done = lag
            source = first - lag * items
            value = u_scr[source:source + count, :]
            if lag == 0:
                matrix = jnp.concatenate([dot(g_scr[at:at + count, :], ones)] * (tile // LANES), axis=1)
                y_scr[first:first + count, :] = (matrix + skip) * value
            else:
                y_scr[first:first + count, :] += dot(g_scr[at:at + count, :], table) * value
        tall = parts * items
        for part in range(parts):
            for column in range(columns):
                here = slice((part * columns + column) * items, (part * columns + column + 1) * items)
                there = slice(column * LANES, (column + 1) * LANES)
                for at in range(tile // LANES):
                    begin = at * tall + part * items
                    l_scr[begin:begin + items, there] = y_scr[here, at * LANES:(at + 1) * LANES].astype(BF16)
        for k in range(0, columns, 2):
            turned = dot(l_scr[...], lane_ref[:, k * LANES:(k + 2) * LANES])
            for at in range(tile // LANES):
                piece, first = divmod(at, tiles_each)
                begin = (first * columns + k) * items
                for part in range(parts):
                    rows_at = at * tall + part * items
                    for j in range(2):
                        out_scr[tile_id, piece, part, begin + j * items:begin + (j + 1) * items, :] = (
                            turned[rows_at:rows_at + items, j * LANES:(j + 1) * LANES].astype(BF16)
                        )
        for piece in range(pieces_out):
            send(tile_id, piece).start()

    for tile_id in range(halves):
        one_tile(tile_id, u_all.at[tile_id], y_all.at[tile_id], l_all.at[tile_id])
    for half in range(halves):
        for piece in range(pieces_out):
            send(half, piece).wait()


def row_scan(x, columns, halves, gain, w_u, w_bc, rate, skip):
    parts, block, width = x.shape
    items = block // columns
    inner = w_u.shape[1]
    state = rate.shape[0]
    rows = parts * block
    w_b, w_c = w_bc[:, :state], w_bc[:, state:2 * state]
    blank = jnp.zeros((width, LANES - 2 * state), BF16)
    w_mix = jnp.concatenate([w_b, w_b, blank, w_c, w_c, blank], axis=1)
    tile = inner // halves
    out_rows = tile * columns // LANES * items
    pieces_out = 2
    out = pl.pallas_call(
        functools.partial(row_kernel, parts, items, columns, halves),
        name="row_scan",
        out_shape=jax.ShapeDtypeStruct((parts, halves, out_rows, LANES), BF16),
        in_specs=[VMEM] * 7,
        out_specs=pl.BlockSpec(memory_space=pltpu.HBM),
        scratch_shapes=[
            pltpu.VMEM((rows, width), BF16),
            pltpu.VMEM((rows, 2 * state), F32),
            pltpu.VMEM((rows, 2 * state), F32),
            pltpu.VMEM((halves, rows, tile), F32),
            pltpu.VMEM((halves, rows, tile), F32),
            pltpu.VMEM((rows * (parts * columns + 1) // 2, 2 * state), BF16),
            pltpu.VMEM((halves, parts * items * tile // LANES, columns * LANES), BF16),
            pltpu.VMEM((halves, pieces_out, parts, out_rows // pieces_out, LANES), BF16),
            pltpu.VMEM((width // LANES, rows, LANES), F32),
            pltpu.SemaphoreType.DMA((halves, pieces_out)),
        ],
        compiler_params=params(20),
        cost_estimate=pl.CostEstimate(
            flops=2 * rows * width * inner * 16, bytes_accessed=4 << 20, transcendentals=0
        ),
    )(x, gain[None, :], w_u, w_mix, rate, skip[None, :], lane_order(columns))
    return out.reshape(parts * halves, out_rows, LANES)


def home_kernel(columns, halves, gain_ref, wz_ref, wm_ref, order_ref, lane_ref, table_ref, *refs):
    x_refs, (gate_ref, mix_ref, n_scr) = refs[:halves], refs[halves:]
    block = order_ref.shape[0]
    items = block // columns
    steps = x_refs[0].shape[0] // columns
    groups = gate_ref.shape[1] // steps
    for half, x_ref in enumerate(x_refs):
        for start in range(x_ref.shape[0] // block):
            here = normalise(x_ref[start * block:(start + 1) * block, :], gain_ref[...])
            here = dot(order_ref[...], here).astype(BF16)
            for column in range(columns):
                first = column * steps + start * items
                n_scr[first:first + items, :] = here[column * items:(column + 1) * items]
        mix = None
        project = []
        for column in range(columns):
            here = n_scr[column * steps:(column + 1) * steps, :]
            project.append(dot(here, wz_ref[...]).astype(BF16))
            part = dot(dot(here, wm_ref[...]).astype(BF16), table_ref[column])
            mix = part if mix is None else mix + part
        for n in range(mix_ref.shape[2]):
            for at in range(steps // items):
                mix_ref[half, at, n] = mix[at * items:(at + 1) * items, n * LANES:(n + 1) * LANES]
        for at in range(wz_ref.shape[1] // LANES):
            joined = jnp.concatenate([part[:, at * LANES:(at + 1) * LANES] for part in project], axis=1)
            gate = dot(joined, lane_ref[...])
            gate = gate / (1.0 + jnp.exp(-gate))
            for k in range(columns):
                gate_ref[half, pl.ds(at * columns + k, steps, stride=groups), :] = gate[:, k * LANES:(k + 1) * LANES]


def home(tokens, items, columns, gain, w_z, w_m):
    halves = len(tokens)
    rows, width = tokens[0].shape
    steps = rows // columns
    groups = w_z.shape[1] * columns // LANES
    count = w_m.shape[1]
    gate, mix = pl.pallas_call(
        functools.partial(home_kernel, columns, halves),
        name="home",
        out_shape=(
            jax.ShapeDtypeStruct((halves, steps * groups, LANES), F32),
            jax.ShapeDtypeStruct((halves, steps // items, count, items, LANES), F32),
        ),
        in_specs=[VMEM] * (6 + halves),
        out_specs=(VMEM, VMEM),
        scratch_shapes=[pltpu.VMEM((rows, width), BF16)],
        compiler_params=params(20),
        cost_estimate=pl.CostEstimate(
            flops=4 * halves * rows * width * w_z.shape[1], bytes_accessed=8 << 20, transcendentals=0
        ),
    )(gain[None, :], w_z, w_m, row_order(items, columns), lane_order(columns), lane_table(columns, count), *tokens)
    return gate.reshape(halves, steps, groups, LANES), mix


def col_kernel(state, halves, core_ref, y_hbm, gate_hbm, mix_hbm, rate_hbm, *rest):
    outs = rest[:halves]
    y_ref, gate_ref, mix_ref, out_ref, held, decay, v_scr, g_scr, sems = rest[halves:]
    per_half, _, span_steps, _ = mix_hbm.shape[1:]
    count = halves * per_half
    groups = gate_hbm.shape[2]
    tiles = groups // 8
    spans = [slice(f * 8, f * 8 + 8) for f in range(tiles)]

    def slot_of(at):
        return lax.rem(at // per_half + halves - core_ref[0], halves)

    def copies(at):
        half, place, slot = at // per_half, at % per_half, slot_of(at)
        first = pl.multiple_of(place * span_steps, span_steps)
        return (
            pltpu.make_async_copy(y_hbm.at[place * halves + half], y_ref.at[at], sems.at[at, 0]),
            pltpu.make_async_copy(mix_hbm.at[slot, place], mix_ref.at[at], sems.at[at, 1]),
            pltpu.make_async_copy(gate_hbm.at[slot, pl.ds(first, span_steps)], gate_ref.at[at], sems.at[at, 2]),
        )

    def result(at, s):
        return pltpu.make_async_copy(out_ref.at[at], outs[s].at[at % per_half], sems.at[at, 3])

    def launch(at, _):
        for copy in copies(at):
            copy.start()
        return 0

    first_copy = pltpu.make_async_copy(rate_hbm, decay, sems.at[count, 0])
    first_copy.start()
    lax.fori_loop(0, min(AHEAD, count), launch, 0)
    held[...] = jnp.zeros_like(held)
    first_copy.wait()
    decay[...] = jnp.exp(-decay[...])

    def one_span(at, _):
        for copy in copies(at):
            copy.wait()

        @pl.when(at + AHEAD < count)
        def _():
            launch(at + AHEAD, 0)

        v_scr[...] = y_ref[at].astype(F32)
        carry = [held[n, span, :] for n in range(state) for span in spans]
        for t in range(span_steps):
            value = [v_scr[pl.ds(f * 8 * span_steps + t, 8, stride=span_steps), :] for f in range(tiles)]
            total = list(value)
            for n in range(state):
                b = jnp.broadcast_to(mix_ref[at, n, t:t + 1, :], (8, LANES))
                c = jnp.broadcast_to(mix_ref[at, state + n, t:t + 1, :], (8, LANES))
                for f, span in enumerate(spans):
                    h = decay[n, span, :] * carry[n * tiles + f] + b * value[f]
                    total[f] = total[f] + c * h
                    carry[n * tiles + f] = h
            for f, span in enumerate(spans):
                g_scr[pl.ds(f * 8 * span_steps + t, 8, stride=span_steps), :] = total[f] * gate_ref[at, t, span, :]
        for n in range(state):
            for f, span in enumerate(spans):
                held[n, span, :] = carry[n * tiles + f]
        out_ref[at] = g_scr[...].astype(BF16)
        for s in range(halves):
            @pl.when(slot_of(at) == s)
            def _(s=s):
                result(at, s).start()
        return 0

    lax.fori_loop(0, count, one_span, 0)

    def finish(at, _):
        for s in range(halves):
            @pl.when(slot_of(at) == s)
            def _(s=s):
                result(at, s).wait()
        return 0

    lax.fori_loop(0, count, finish, 0)


def col_scan(core, y, gate, mix, rate):
    state, groups, _ = rate.shape
    halves, per_half, _, span_steps, _ = mix.shape
    count = halves * per_half
    far = pl.BlockSpec(memory_space=pltpu.HBM)
    return pl.pallas_call(
        functools.partial(col_kernel, state, halves),
        name="col_scan",
        in_specs=[pl.BlockSpec(memory_space=pltpu.SMEM)] + [far] * 4,
        out_specs=[far] * halves,
        scratch_shapes=[
            pltpu.VMEM((count, groups * span_steps, LANES), BF16),
            pltpu.VMEM((count, span_steps, groups, LANES), F32),
            pltpu.VMEM((count, 2 * state, span_steps, LANES), F32),
            pltpu.VMEM((count, groups * span_steps, LANES), BF16),
            pltpu.VMEM(rate.shape, F32),
            pltpu.VMEM(rate.shape, F32),
            pltpu.VMEM((span_steps * groups, LANES), F32),
            pltpu.VMEM((span_steps * groups, LANES), F32),
            pltpu.SemaphoreType.DMA((count + 1, 4)),
        ],
        out_shape=[jax.ShapeDtypeStruct((per_half, groups * span_steps, LANES), BF16)] * halves,
        compiler_params=params(62),
        cost_estimate=pl.CostEstimate(flops=5 * count * span_steps * groups * LANES * state,
                                      bytes_accessed=8 << 20, transcendentals=0),
    )(core, y, gate, mix, rate)


def last_kernel(columns, halves, group_ref, part_ref, w_ref, lane_ref, *refs):
    out_ref, l_scr = refs[-2:]
    spans, rows, _ = part_ref.shape
    width = w_ref.shape[0] // halves
    groups = width * columns // LANES
    span = rows // groups
    steps = spans * span
    for at in range(width // LANES):
        joined = jnp.concatenate([
            jnp.concatenate([
                part_ref[p, (at * columns + k) * span:(at * columns + k + 1) * span, :] for p in range(spans)
            ], axis=0) for k in range(columns)
        ], axis=1)
        turned = dot(joined, lane_ref[...])
        for column in range(columns):
            l_scr[at, pl.ds(column, steps, stride=columns), :] = turned[:, column * LANES:(column + 1) * LANES]
    first = pl.multiple_of(group_ref[0] * width, width)
    gated = jnp.concatenate([l_scr[at].astype(BF16) for at in range(width // LANES)], axis=1)
    total = dot(gated, w_ref[pl.ds(first, width), :])
    if len(refs) > 2:
        total = total + refs[0][...]
    out_ref[...] = total.reshape(out_ref.shape).astype(out_ref.dtype)


def last(group, part, w_out, columns, halves, before, out_type):
    inner, features = w_out.shape
    groups = inner * columns // (halves * LANES)
    steps = part.shape[0] * part.shape[1] // groups
    rows = steps * columns
    others = () if before is None else (before,)
    return pl.pallas_call(
        functools.partial(last_kernel, columns, halves),
        name="last",
        out_shape=jax.ShapeDtypeStruct((steps, columns, features) if out_type == BF16 else (rows, features), out_type),
        in_specs=[pl.BlockSpec(memory_space=pltpu.SMEM)] + [VMEM] * (3 + len(others)),
        out_specs=VMEM,
        scratch_shapes=[pltpu.VMEM((groups // columns, rows, LANES), F32)],
        compiler_params=params(8),
        cost_estimate=pl.CostEstimate(
            flops=2 * rows * features * groups * LANES // columns, bytes_accessed=2 << 20, transcendentals=0
        ),
    )(group.reshape(1), part, w_out, lane_order(columns).T, *others)


def wide_row_scan(x, columns, halves, gain, w_u, w_bc, rate, skip):
    parts, block, width = x.shape
    items = block // columns
    inner = w_u.shape[1]
    state = rate.shape[0]
    normed = normalise(x.reshape(parts, items, columns, width), gain)
    normed = normed.transpose(0, 2, 1, 3).reshape(parts * columns, items, width)
    value = dot(normed, w_u).astype(BF16).astype(F32)
    mix = dot(normed, w_bc).astype(BF16).astype(F32)
    factor = jnp.exp(-rate)

    def advance(held, now):
        value_now, inject, readout = now
        held = factor * held + inject[:, :, None] * value_now[:, None, :]
        return held, jnp.sum(held * readout[:, :, None], axis=1) + skip * value_now

    start = jnp.zeros((items, state, inner), F32)
    _, out = lax.scan(advance, start, (value, mix[..., :state], mix[..., state:2 * state]))
    lanes = LANES // columns
    out = out.astype(BF16).reshape(parts, columns, items, halves, inner // (halves * lanes), lanes)
    return out.transpose(0, 3, 4, 2, 1, 5).reshape(parts * halves, -1, LANES)


def per_device(tokens, norm_gain, w_in, w_bc, rate_row, rate_col, skip_gain, w_out):
    height, columns, features = tokens.shape
    inner = w_out.shape[0]
    state = rate_row.shape[0]
    parts, halves = lax.axis_size("rows"), lax.axis_size("cols")
    core = lax.axis_index("cols")
    both = ("rows", "cols")
    items = height // parts
    group = inner // halves
    lanes = LANES // columns
    moved = lax.all_to_all(
        tokens.reshape(parts, items, columns, features), "rows", split_axis=0, concat_axis=0, tiled=True
    )
    scan = row_scan if items == SPAN and parts * columns <= 64 else wide_row_scan
    row_mixed = scan(
        moved.reshape(parts, items * columns, features), columns, halves, norm_gain,
        w_in[:, :inner], w_bc[:, :2 * state], rate_row, skip_gain
    )
    back = lax.all_to_all(row_mixed, both, split_axis=0, concat_axis=0, tiled=True)

    tokens = tokens.reshape(height * columns, features)
    whole = [tokens] + [
        lax.ppermute(tokens, "cols", [(k, (k - s) % halves) for k in range(halves)]) for s in range(1, halves)
    ]
    own = core * group
    w_gate = lax.dynamic_slice_in_dim(w_in, inner + own, group, 1)
    gate, mix = home(whole, SPAN, columns, norm_gain, w_gate, w_bc[:, 2 * state:])
    rate = lax.dynamic_slice_in_dim(rate_col, own, group, 1)
    rate = jnp.tile(rate.reshape(state, group // lanes, lanes), (1, 1, columns))
    if items != SPAN:
        spans = height // SPAN
        back = back.reshape(spans, parts // spans, halves, group // lanes, items, LANES)
        back = back.transpose(0, 2, 3, 1, 4, 5).reshape(spans * halves, -1, LANES)
    gated = col_scan(core.reshape(1), back, gate, mix, rate)
    out = last(core, gated[0], w_out, columns, halves, None, BF16 if halves == 1 else F32)
    for s in range(1, halves):
        arrived = lax.ppermute(gated[s], "cols", [(k, (k + s) % halves) for k in range(halves)])
        out = last((core - s) % halves, arrived, w_out, columns, halves, out, BF16 if s == halves - 1 else F32)
    return out


def solution(mesh):
    placed = (P(("slides", "cols"), "rows", None), P(), P(), P(), P(), P(), P(), P())
    return jax.shard_map(
        per_device,
        mesh=mesh,
        in_specs=placed,
        out_specs=P(("slides", "cols"), "rows", None),
        check_vma=False,
    )
```
